256 devices in a mesh: seq: 16 (over y, x), ctx: 16 (over z, core).
Axes of the slice: x: 4, y: 4, z: 8, core: 2. Of those that a mesh axis runs over, the one named last changes fastest.
Arguments:
- queries: bfloat16 [16, 2048, 2048], P('ctx', 'seq'), may hold values from -30 to 30
- keys: bfloat16 [16, 2048, 2048], P('ctx', 'seq'), may hold values from -30 to 30
- values: bfloat16 [16, 2048, 2048], P('ctx', 'seq'), may hold values from -6 to 6
- out_grad: bfloat16 [16, 2048, 2048], P('ctx', 'seq'), may hold values from -6 to 6
- tile_mask: int32 [16, 16, 16, 256], P('seq'), may hold values from 0 to 1, as said below
Outputs:
- attended: bfloat16 [16, 2048, 2048], P('ctx', 'seq')
- query_grad: bfloat16 [16, 2048, 2048], P('ctx', 'seq')
- key_grad: bfloat16 [16, 2048, 2048], P('ctx', 'seq')
- value_grad: bfloat16 [16, 2048, 2048], P('ctx', 'seq')
The draws below stay inside these ranges and needn't reach their ends.
Inputs may be any that keep to these rules, and one draw needn't show every extreme that they name: tile_mask[h, f, i, t] is 1 only where the key tile t lies in frame f - 1, f or f + 1; every query tile attends its own tile; a query tile attends at most 18 key tiles and some query tile attends exactly 18.
All inputs are finite; a program needn't handle non-finite values.
Results may differ from the reference program's by a relative error of at most 0.025.
Values may be sent and summed in bfloat16 or wider, within the bound.
A program may use at most 128 MiB of HBM per device.

```python
import jax
import jax.numpy as jnp
from jax import lax

HD = 128
HEADS = 16
TILE = 128
FT = 2048
FRAMES = 16
TW = 8
RT = 16
KT = 256
KMAX = 18


def draw_queries(key, part):
    key = jax.random.fold_in(key, 11)
    result = jax.random.normal(key, (FRAMES, FT, HEADS, HD), jnp.float32)
    return jnp.clip(result, -30.0, 30.0).reshape(FRAMES, FT, HEADS * HD).astype(jnp.bfloat16)


def draw_keys(key, part):
    key = jax.random.fold_in(key, 13)
    result = jax.random.normal(key, (FRAMES, FT, HEADS, HD), jnp.float32)
    return jnp.clip(result, -30.0, 30.0).reshape(FRAMES, FT, HEADS * HD).astype(jnp.bfloat16)


def draw_tile_mask(key, part):
    key = jax.random.fold_in(key, 17)
    radii = jax.random.randint(key, (HEADS, FRAMES, 3), 0, 2, jnp.int32)
    radii = radii.at[0, 1].set(1)
    query_tile = jnp.arange(RT, dtype=jnp.int32)
    key_tile = jnp.arange(KT, dtype=jnp.int32)
    frame_q = jnp.arange(FRAMES, dtype=jnp.int32)[None, :, None, None]
    frame_k = (key_tile // RT)[None, None, None, :]
    row_q = (query_tile // TW)[None, None, :, None]
    col_q = (query_tile % TW)[None, None, :, None]
    row_k = (key_tile % RT // TW)[None, None, None, :]
    col_k = (key_tile % RT % TW)[None, None, None, :]
    reach_t = radii[:, :, 0][:, :, None, None]
    reach_h = radii[:, :, 1][:, :, None, None]
    reach_w = radii[:, :, 2][:, :, None, None]
    inside = (jnp.abs(frame_k - frame_q) <= reach_t) & (jnp.abs(row_k - row_q) <= reach_h) & (jnp.abs(col_k - col_q) <= reach_w)
    return inside.astype(jnp.int32)


def block_levels(rng, extent, shards, smallest, top_value):
    def one(axis_at, blocks):
        steps = jax.random.uniform(jax.random.fold_in(jax.random.fold_in(rng, 6), axis_at), (blocks,), jnp.float32, smallest / len(shards), top_value / len(shards))
        return jnp.repeat(jnp.exp(steps), extent[axis_at] // blocks).reshape((-1,) + (1,) * (len(extent) - axis_at - 1))

    loudness = one(*shards[0])
    for cut in shards[1:]:
        loudness = loudness * one(*cut)
    return loudness


def scatter_about(key, shape, scale, bound, cuts=(), held_as=jnp.bfloat16):
    values = jax.random.normal(key, shape, jnp.float32) * scale
    if len(cuts) > 0:
        values = block_levels(key, shape, cuts, -0.22, 0.18) * values
    return jnp.clip(values, min=-bound, max=bound).astype(held_as)


def setup_inputs(seed: int = 0) -> dict:
    streams_of = jax.random.split(jax.random.key(seed), 6)
    return {
        "queries": draw_queries(jax.random.fold_in(streams_of[5], 71), 0),
        "keys": draw_keys(jax.random.fold_in(streams_of[5], 71), 0),
        "values": scatter_about(streams_of[2], (FRAMES, FT, HEADS * HD), 1.0, 6.0, ((0, 16), (1, 16))),
        "out_grad": scatter_about(streams_of[3], (FRAMES, FT, HEADS * HD), 1.0, 6.0, ((0, 16), (1, 16))),
        "tile_mask": draw_tile_mask(jax.random.fold_in(streams_of[5], 71), 0),
    }


masked_score = -1.0e30


def key_lists(mask_rows, slot_count):
    columns = mask_rows.shape[-1]
    ranking = mask_rows * (2 * columns) + (columns - 1 - jnp.arange(columns, dtype=jnp.int32))
    _, chosen = lax.top_k(ranking, slot_count)
    chosen = chosen.astype(jnp.int32)
    return chosen, jnp.take_along_axis(mask_rows, chosen, axis=-1)


def tile_terms(keys3, values3, query, grad_out, chosen, present):
    scaling = HD ** -0.5
    gathered_keys = keys3[chosen].reshape(-1, HD)
    gathered_values = values3[chosen].reshape(-1, HD)
    allowed = (jnp.repeat(present, TILE) > 0)[None, :]
    logits = jnp.dot(query, gathered_keys.T, preferred_element_type=jnp.float32) * scaling
    logits = jnp.where(allowed, logits, masked_score)
    highest = jnp.max(logits, axis=1, keepdims=True)
    log_total = highest + jnp.log(jnp.sum(jnp.exp(logits - highest), axis=1, keepdims=True))
    weights = jnp.where(allowed, jnp.exp(logits - log_total), 0.0)
    weights_b = weights.astype(jnp.bfloat16)
    attended = jnp.dot(weights_b, gathered_values, preferred_element_type=jnp.float32).astype(jnp.bfloat16)
    row_dot = jnp.sum(grad_out.astype(jnp.float32) * attended.astype(jnp.float32), axis=1, keepdims=True)
    weight_grad = jnp.dot(grad_out, gathered_values.T, preferred_element_type=jnp.float32)
    logit_grad = (weights * (weight_grad - row_dot)).astype(jnp.bfloat16)
    query_grad = (jnp.dot(logit_grad, gathered_keys, preferred_element_type=jnp.float32) * scaling).astype(jnp.bfloat16)
    key_terms = jnp.dot(logit_grad.T, query, preferred_element_type=jnp.float32) * scaling
    value_terms = jnp.dot(weights_b.T, grad_out, preferred_element_type=jnp.float32)
    return attended, query_grad, key_terms.reshape(-1, TILE, HD), value_terms.reshape(-1, TILE, HD)


def one_head(head_queries, head_keys, head_values, head_grads, head_mask):
    pad_frames = ((1, 1), (0, 0), (0, 0))
    keys_padded = jnp.pad(head_keys, pad_frames)
    values_padded = jnp.pad(head_values, pad_frames)
    mask_padded = jnp.pad(head_mask, ((0, 0), (0, 0), (RT, RT)))

    def per_frame(carry, frame_at):
        key_total, value_total = carry
        keys3 = lax.dynamic_slice_in_dim(keys_padded, frame_at, 3, 0).reshape(3 * RT, TILE, HD)
        values3 = lax.dynamic_slice_in_dim(values_padded, frame_at, 3, 0).reshape(3 * RT, TILE, HD)
        mask_rows = lax.dynamic_index_in_dim(mask_padded, frame_at, 0, keepdims=False)
        window = lax.dynamic_slice_in_dim(mask_rows, frame_at * RT, 3 * RT, 1)
        chosen, present = key_lists(window, KMAX)
        query_tiles = lax.dynamic_index_in_dim(head_queries, frame_at, 0, keepdims=False).reshape(RT, TILE, HD)
        grad_tiles = lax.dynamic_index_in_dim(head_grads, frame_at, 0, keepdims=False).reshape(RT, TILE, HD)
        attended, query_grad, key_terms, value_terms = jax.vmap(tile_terms, in_axes=(None, None, 0, 0, 0, 0))(
            keys3, values3, query_tiles, grad_tiles, chosen, present)
        flat_chosen = chosen.reshape(-1)
        key_near = jnp.zeros((3 * RT, TILE, HD), jnp.float32).at[flat_chosen].add(
            key_terms.reshape(-1, TILE, HD)).reshape(3, FT, HD)
        value_near = jnp.zeros((3 * RT, TILE, HD), jnp.float32).at[flat_chosen].add(
            value_terms.reshape(-1, TILE, HD)).reshape(3, FT, HD)
        key_total = lax.dynamic_update_slice_in_dim(
            key_total, lax.dynamic_slice_in_dim(key_total, frame_at, 3, 0) + key_near, frame_at, 0)
        value_total = lax.dynamic_update_slice_in_dim(
            value_total, lax.dynamic_slice_in_dim(value_total, frame_at, 3, 0) + value_near, frame_at, 0)
        return (key_total, value_total), (attended.reshape(FT, HD), query_grad.reshape(FT, HD))

    zero_total = jnp.zeros((FRAMES + 2, FT, HD), jnp.float32)
    (key_total, value_total), (attended, query_grad) = lax.scan(
        per_frame, (zero_total, zero_total), jnp.arange(FRAMES, dtype=jnp.int32))
    return attended, query_grad, key_total[1:-1].astype(jnp.bfloat16), value_total[1:-1].astype(jnp.bfloat16)


def head_first(stacked_in):
    return stacked_in.reshape(FRAMES, FT, HEADS, HD).transpose(2, 0, 1, 3)


def token_first(stacked_out):
    return stacked_out.transpose(1, 2, 0, 3).reshape(FRAMES, FT, HEADS * HD)


def reference(queries, keys, values, out_grad, tile_mask):
    results = lax.map(lambda operands: one_head(*operands),
                      (head_first(queries), head_first(keys), head_first(values), head_first(out_grad), tile_mask))
    return token_first(results[0]), token_first(results[1]), token_first(results[2]), token_first(results[3])
```

```python
import functools

import jax
import jax.numpy as jnp
from jax import lax
from jax.experimental import pallas as pl
from jax.experimental.pallas import tpu as pltpu
from jax.sharding import PartitionSpec as P

MESH = pl.DeviceIdType.MESH
HD = 128
LOG2E = 1.4426950408889634
NEG = -1e30


def dot_nt(a, b):
    return lax.dot_general(a, b, (((1,), (1,)), ((), ())), preferred_element_type=jnp.float32)


def dot_nn(a, b):
    return lax.dot_general(a, b, (((1,), (0,)), ((), ())), preferred_element_type=jnp.float32)


def kernel(
    rows, cols, slots, groups, frames,
    ci, bias, gp, gq, keep, last,
    q_in, k_in, v_in, g_in,
    o_out, dq_out, dk_out, dv_out,
    k3, v3, qh, gh, sbuf, pst, dst, qt, gt, park, parv, ot, dqt, snd, rcv, dkt, dvt,
    in_send, in_recv, in_local, halo_send, halo_recv, gr_send, gr_recv, out_send, out_recv, out_local,
):
    n = rows * cols
    me = lax.axis_index("seq")
    frame = lax.axis_index("ctx")
    my_row, my_col = me // cols, me % cols
    has_prev, has_next = frame > 0, frame < frames - 1

    def peer(r, sign):
        dr, dc = r // cols, r % cols
        row = lax.rem(my_row + sign * dr + rows, rows)
        col = lax.rem(my_col + sign * dc + cols, cols)
        return row * cols + col

    barrier = pltpu.get_barrier_semaphore()

    def greet(r, _):
        pl.semaphore_signal(barrier, inc=1, device_id=(peer(r, 1), frame), device_id_type=MESH)
        return 0

    lax.fori_loop(1, n, greet, 0)

    for step in (1, frames - 1):
        beside = lax.rem(frame + step, frames)
        pl.semaphore_signal(barrier, inc=1, device_id=(me, beside), device_id_type=MESH)
    pl.semaphore_wait(barrier, n + 1)

    arrays = ((k_in, k3, n), (v_in, v3, n), (q_in, qh, 0), (g_in, gh, 0))

    def in_copy(a, target, source):
        src, dst_ref, base = arrays[a]
        return pltpu.make_async_remote_copy(
            src_ref=src.at[0, :, pl.ds(pl.multiple_of(target * HD, HD), HD)],
            dst_ref=dst_ref.at[base + source],
            send_sem=in_send.at[a, target],
            recv_sem=in_recv.at[a, source],
            device_id=(target, frame),
            device_id_type=MESH,
        )

    def in_own(a):
        src, dst_ref, base = arrays[a]
        return pltpu.make_async_copy(
            src.at[0, :, pl.ds(pl.multiple_of(me * HD, HD), HD)],
            dst_ref.at[base + me],
            in_local.at[a],
        )

    for a in range(4):
        in_own(a).start()

        def send(r, _, a=a):
            in_copy(a, peer(r, 1), me).start()
            return 0

        lax.fori_loop(1, n, send, 0)

    def halo_copy(a, side):
        ref = (k3, v3)[a]
        return pltpu.make_async_remote_copy(
            src_ref=ref.at[pl.ds(n, n)],
            dst_ref=ref.at[pl.ds(2 * n if side == 0 else 0, n)],
            send_sem=halo_send.at[a, side],
            recv_sem=halo_recv.at[a, side],
            device_id=(me, frame - 1 if side == 0 else frame + 1),
            device_id_type=MESH,
        )

    sides = ((0, has_prev, has_next), (1, has_next, has_prev))
    zero_tile = jnp.zeros((HD, HD), jnp.bfloat16)
    pst[n * slots] = zero_tile
    dst[n * slots] = zero_tile
    park[groups] = zero_tile
    parv[groups] = zero_tile

    @pl.when(jnp.logical_not(has_prev))
    def _():
        k3[0:n] = jnp.zeros((n, HD, HD), jnp.bfloat16)
        v3[0:n] = jnp.zeros((n, HD, HD), jnp.bfloat16)
        rcv[1] = jnp.zeros(rcv.shape[1:], jnp.bfloat16)

    @pl.when(jnp.logical_not(has_next))
    def _():
        k3[2 * n : 3 * n] = jnp.zeros((n, HD, HD), jnp.bfloat16)
        v3[2 * n : 3 * n] = jnp.zeros((n, HD, HD), jnp.bfloat16)
        rcv[0] = jnp.zeros(rcv.shape[1:], jnp.bfloat16)

    for a in range(2):
        in_own(a).wait()

        def arrive(r, _, a=a):
            in_copy(a, peer(r, 1), peer(r, -1)).wait_recv()
            return 0

        lax.fori_loop(1, n, arrive, 0)
        for side, send_if, _ in sides:
            @pl.when(send_if)
            def _(a=a, side=side):
                halo_copy(a, side).start()

    for a in range(2):
        for side, _, recv_if in sides:
            @pl.when(recv_if)
            def _(a=a, side=side):
                halo_copy(a, side).wait_recv()

    half = slots // 2
    scale = HD ** -0.5
    out_arrays = ((ot, o_out), (dqt, dq_out), (dkt, dk_out), (dvt, dv_out))

    def out_copy(a, target, source):
        tiles, out = out_arrays[a]
        return pltpu.make_async_remote_copy(
            src_ref=tiles.at[target],
            dst_ref=out.at[0, :, pl.ds(pl.multiple_of(source * HD, HD), HD)],
            send_sem=out_send.at[a, target],
            recv_sem=out_recv.at[a, source],
            device_id=(target, frame),
            device_id_type=MESH,
        )

    def out_own(a):
        tiles, out = out_arrays[a]
        return pltpu.make_async_copy(
            tiles.at[me],
            out.at[0, :, pl.ds(pl.multiple_of(me * HD, HD), HD)],
            out_local.at[a],
        )

    def pair_of(ref, i, jj):
        return jnp.concatenate([ref[ci[i, 2 * jj]], ref[ci[i, 2 * jj + 1]]], axis=0)

    def query_tile(i):
        q = qh[i]
        g = gh[i]
        gf = g.astype(jnp.float32)
        gt[i] = gf.T.astype(jnp.bfloat16)
        qt[i] = q.astype(jnp.float32).T.astype(jnp.bfloat16)
        top = jnp.full((HD, HD), NEG, jnp.float32)
        for jj in range(half):
            s = dot_nt(q, pair_of(k3, i, jj)) * (scale * LOG2E)
            s0 = s[:, :HD] + bias[i, 2 * jj]
            s1 = s[:, HD:] + bias[i, 2 * jj + 1]
            sbuf[:, jj * 2 * HD : jj * 2 * HD + HD] = s0
            sbuf[:, jj * 2 * HD + HD : (jj + 1) * 2 * HD] = s1
            top = jnp.maximum(top, jnp.maximum(s0, s1))
        highest = jnp.max(top, axis=1, keepdims=True)
        total = jnp.zeros((HD, HD), jnp.float32)
        o = jnp.zeros((HD, HD), jnp.float32)
        for jj in range(half):
            at = slice(jj * 2 * HD, (jj + 1) * 2 * HD)
            p = jnp.exp2(sbuf[:, at] - highest)
            sbuf[:, at] = p
            total = total + (p[:, :HD] + p[:, HD:])
            o = o + dot_nn(p.astype(jnp.bfloat16), pair_of(v3, i, jj))
        inv = 1.0 / jnp.sum(total, axis=1, keepdims=True)
        o = o * inv
        ob = o.astype(jnp.bfloat16)
        ot[i] = ob
        row_dot = jnp.sum(gf * ob.astype(jnp.float32), axis=1, keepdims=True)
        dq = jnp.zeros((HD, HD), jnp.float32)
        for jj in range(half):
            at = slice(jj * 2 * HD, (jj + 1) * 2 * HD)
            p = sbuf[:, at] * inv
            dp = dot_nt(g, pair_of(v3, i, jj))
            ds = (p * (dp - row_dot)).astype(jnp.bfloat16)
            pb = p.astype(jnp.bfloat16)
            dq = dq + dot_nn(ds, pair_of(k3, i, jj))
            base = i * slots + 2 * jj
            pst[base] = pb[:, :HD]
            pst[base + 1] = pb[:, HD:]
            dst[base] = ds[:, :HD]
            dst[base + 1] = ds[:, HD:]
        dqt[i] = (dq * scale).astype(jnp.bfloat16)

    def own_tile():
        for a in (2, 3):
            in_own(a).wait()
        query_tile(me)
        for a in (0, 1):
            out_own(a).start()

    def other_tile(r, _):
        source = peer(r, -1)
        for a in (2, 3):
            in_copy(a, peer(r, 1), source).wait_recv()
        query_tile(source)
        for a in (0, 1):
            out_copy(a, source, me).start()
        return 0

    own_tile()
    lax.fori_loop(1, n, other_tile, 0)

    def group(x, carry):
        acc_k, acc_v = carry
        a, b = gp[2 * x], gp[2 * x + 1]
        qa, qb = gq[2 * x], gq[2 * x + 1]
        hold = keep[x]
        acc_v = acc_v * hold + dot_nn(
            jnp.concatenate([gt[qa], gt[qb]], axis=1), jnp.concatenate([pst[a], pst[b]], axis=0))
        acc_k = acc_k * hold + dot_nn(
            jnp.concatenate([qt[qa], qt[qb]], axis=1), jnp.concatenate([dst[a], dst[b]], axis=0))
        parv[x] = acc_v.astype(jnp.bfloat16)
        park[x] = (acc_k * scale).astype(jnp.bfloat16)
        return acc_k, acc_v

    zero = jnp.zeros((HD, HD), jnp.float32)
    lax.fori_loop(0, groups, group, (zero, zero))

    def tile_of(par, t):
        return par[last[t]].astype(jnp.float32).T

    def gr_copy(a, side, i):
        return pltpu.make_async_remote_copy(
            src_ref=snd.at[side, a, i],
            dst_ref=rcv.at[side, a, i],
            send_sem=gr_send.at[side, a, i],
            recv_sem=gr_recv.at[side, a, i],
            device_id=(me, frame - 1 if side == 0 else frame + 1),
            device_id_type=MESH,
        )

    def neighbour_terms(i, _):
        for side, send_if, _ in sides:
            @pl.when(send_if)
            def _(side=side):
                for a in range(2):
                    t = i if side == 0 else 2 * n + i
                    snd[side, a, i] = tile_of((park, parv)[a], t).astype(jnp.bfloat16)
                    gr_copy(a, side, i).start()
        return 0

    lax.fori_loop(0, n, neighbour_terms, 0)

    def finish(i):
        for side, _, recv_if in sides:
            @pl.when(recv_if)
            def _(side=side):
                for a in range(2):
                    gr_copy(a, side, i).wait_recv()
        for a in range(2):
            tot = tile_of((park, parv)[a], n + i)
            tot = tot + rcv[0, a, i].astype(jnp.float32) + rcv[1, a, i].astype(jnp.float32)
            (dkt, dvt)[a][i] = tot.astype(jnp.bfloat16)

    def finish_other(r, _):
        i = peer(r, -1)
        finish(i)
        for a in (2, 3):
            out_copy(a, i, me).start()
        return 0

    lax.fori_loop(1, n, finish_other, 0)
    finish(me)
    for a in (2, 3):
        out_own(a).start()

    for a in range(4):
        out_own(a).wait()

        def settle(r, _, a=a):
            there, back = peer(r, 1), peer(r, -1)
            in_copy(a, there, me).wait_send()
            out_copy(a, back, me).wait_send()
            out_copy(a, there, back).wait_recv()
            return 0

        lax.fori_loop(1, n, settle, 0)
    for side, send_if, _ in sides:
        @pl.when(send_if)
        def _(side=side):
            for a in range(2):
                halo_copy(a, side).wait_send()

            def settle_terms(i, _):
                for a in range(2):
                    gr_copy(a, side, i).wait_send()
                return 0

            lax.fori_loop(0, n, settle_terms, 0)


def tables(window, slots, groups):
    n, total = window.shape
    w = window > 0
    t = jnp.arange(total, dtype=jnp.int32)
    i = jnp.arange(n, dtype=jnp.int32)
    before = (t[:, None] < t[None, :]).astype(jnp.int32)
    pos = jnp.sum(window[:, :, None] * before[None], axis=1)
    count = jnp.sum(window, axis=1)
    j = jnp.arange(slots, dtype=jnp.int32)
    hit = w[:, None, :] & (pos[:, None, :] == j[None, :, None])
    chosen = jnp.sum(jnp.where(hit, t[None, None, :], 0), axis=2)
    present = j[None, :] < count[:, None]
    chosen = jnp.where(present, chosen, n + i[:, None])
    bias = jnp.where(present, 0.0, NEG).astype(jnp.float32)
    pair = i[:, None] * slots + pos
    number = jnp.sum(window, axis=0)
    rank = jnp.sum(window[:, None, :] * (i[:, None, None] < i[None, :, None]).astype(jnp.int32), axis=0)
    used = (number + 1) // 2
    start = jnp.sum(used[:, None] * before, axis=0)
    place = jnp.where(w, 2 * start[None, :] + rank, -1)
    x = jnp.arange(2 * groups, dtype=jnp.int32)
    found = place.reshape(1, -1) == x[:, None]
    gp = jnp.sum(jnp.where(found, pair.reshape(1, -1) - n * slots, 0), axis=1) + n * slots
    gq = jnp.minimum(gp // slots, n - 1)
    opens = jnp.any((start[None, :] == jnp.arange(groups)[:, None]) & (number > 0)[None, :], axis=1)
    keep = jnp.where(opens, 0.0, 1.0).astype(jnp.float32)
    last = jnp.where(number > 0, start + used - 1, groups)
    return chosen, bias, gp, gq, keep, last


def body(shape, queries, keys, values, out_grad, tile_mask):
    rows, cols, frames = shape
    n = rows * cols
    slots = min(18, 3 * n)
    groups = (n * slots + 3 * n) // 2
    frame = lax.axis_index("ctx")
    padded = jnp.pad(tile_mask[0], ((0, 0), (0, 0), (n, n)))
    own = lax.dynamic_index_in_dim(padded, frame, 0, keepdims=False)
    window = lax.dynamic_slice_in_dim(own, frame * n, 3 * n, 1)
    lists = tables(window, slots, groups)
    smem = pl.BlockSpec(memory_space=pltpu.SMEM)
    any_ = pl.BlockSpec(memory_space=pl.ANY)
    tile = lambda *lead: pltpu.VMEM(lead + (HD, HD), jnp.bfloat16)
    dma = pltpu.SemaphoreType.DMA
    return pl.pallas_call(
        functools.partial(kernel, rows, cols, slots, groups, frames),
        out_shape=[jax.ShapeDtypeStruct(queries.shape, jnp.bfloat16)] * 4,
        in_specs=[smem] * 6 + [any_] * 4,
        out_specs=[any_] * 4,
        scratch_shapes=[
            tile(3 * n), tile(3 * n), tile(n), tile(n),
            pltpu.VMEM((HD, slots * HD), jnp.float32),
            tile(n * slots + 1), tile(n * slots + 1),
            tile(n), tile(n),
            tile(groups + 1), tile(groups + 1),
            tile(n), tile(n), tile(2, 2, n), tile(2, 2, n), tile(n), tile(n),
            dma((4, n)), dma((4, n)), dma((4,)),
            dma((2, 2)), dma((2, 2)),
            dma((2, 2, n)), dma((2, 2, n)),
            dma((4, n)), dma((4, n)), dma((4,)),
        ],
        compiler_params=pltpu.CompilerParams(
            collective_id=0, has_side_effects=True, vmem_limit_bytes=56 * 1024 * 1024),
    )(*lists, queries, keys, values, out_grad)


def solution(mesh):
    n, frames = mesh.shape["seq"], mesh.shape["ctx"]
    cols = 4 if n % 4 == 0 and n > 4 else 2
    shape = (n // cols, cols, frames)
    data = P("ctx", "seq", None)
    return jax.shard_map(
        functools.partial(body, shape),
        mesh=mesh,
        in_specs=(data,) * 4 + (P("seq", None, None, None),),
        out_specs=(data,) * 4,
        check_vma=False,
    )
```

```python
import functools

import jax
import jax.numpy as jnp
from jax import lax
from jax.experimental import pallas as pl
from jax.experimental.pallas import tpu as pltpu
from jax.sharding import PartitionSpec as P

MESH = pl.DeviceIdType.MESH
HD = 128
LOG2E = 1.4426950408889634
NEG = -1e30
BLOCK = 4


def dot_nt(a, b):
    return lax.dot_general(a, b, (((1,), (1,)), ((), ())), preferred_element_type=jnp.float32)


def dot_nn(a, b):
    return lax.dot_general(a, b, (((1,), (0,)), ((), ())), preferred_element_type=jnp.float32)


def together(*parts):
    parts = list(parts)
    while parts:
        for part in list(parts):
            if next(part, True):
                parts.remove(part)


def kernel(
    rows, cols, slots, groups, frames,
    ci, bias, gp, gq, keep, last,
    q_in, k_in, v_in, g_in,
    o_out, dq_out, dk_out, dv_out,
    k3, v3, qh, gh, sbuf, pst, dst, qt, gt, park, parv, ot, dqt, snd, rcv, dkt, dvt,
    in_send, in_recv, in_local, halo_send, halo_recv, gr_send, gr_recv, out_send, out_recv, out_local,
):
    n = rows * cols
    me = lax.axis_index("seq")
    frame = lax.axis_index("ctx")
    my_row, my_col = me // cols, me % cols
    has_prev, has_next = frame > 0, frame < frames - 1

    def peer(r, sign):
        dr, dc = r // cols, r % cols
        row = lax.rem(my_row + sign * dr + rows, rows)
        col = lax.rem(my_col + sign * dc + cols, cols)
        return row * cols + col

    barrier = pltpu.get_barrier_semaphore()

    def greet(r, _):
        pl.semaphore_signal(barrier, inc=1, device_id=(peer(r, 1), frame), device_id_type=MESH)
        return 0

    lax.fori_loop(1, n, greet, 0)

    for step in (1, frames - 1):
        beside = lax.rem(frame + step, frames)
        pl.semaphore_signal(barrier, inc=1, device_id=(me, beside), device_id_type=MESH)
    pl.semaphore_wait(barrier, n + 1)

    arrays = ((k_in, k3, n), (v_in, v3, n), (q_in, qh, 0), (g_in, gh, 0))

    def in_copy(a, target, source):
        src, dst_ref, base = arrays[a]
        return pltpu.make_async_remote_copy(
            src_ref=src.at[0, :, pl.ds(pl.multiple_of(target * HD, HD), HD)],
            dst_ref=dst_ref.at[base + source],
            send_sem=in_send.at[a, target],
            recv_sem=in_recv.at[a, source],
            device_id=(target, frame),
            device_id_type=MESH,
        )

    def in_own(a):
        src, dst_ref, base = arrays[a]
        return pltpu.make_async_copy(
            src.at[0, :, pl.ds(pl.multiple_of(me * HD, HD), HD)],
            dst_ref.at[base + me],
            in_local.at[a],
        )

    for a in range(4):
        in_own(a).start()

        def send(r, _, a=a):
            in_copy(a, peer(r, 1), me).start()
            return 0

        lax.fori_loop(1, n, send, 0)

    def halo_copy(a, side, chunk):
        ref = (k3, v3)[a]
        first = chunk * cols
        return pltpu.make_async_remote_copy(
            src_ref=ref.at[pl.ds(n + first, cols)],
            dst_ref=ref.at[pl.ds((2 * n if side == 0 else 0) + first, cols)],
            send_sem=halo_send.at[a, side, chunk],
            recv_sem=halo_recv.at[a, side, chunk],
            device_id=(me, frame - 1 if side == 0 else frame + 1),
            device_id_type=MESH,
        )

    sides = ((0, has_prev, has_next), (1, has_next, has_prev))
    zero_tile = jnp.zeros((HD, HD), jnp.bfloat16)
    pst[n * slots] = zero_tile
    dst[n * slots] = zero_tile
    park[groups] = zero_tile
    parv[groups] = zero_tile

    @pl.when(jnp.logical_not(has_prev))
    def _():
        k3[0:n] = jnp.zeros((n, HD, HD), jnp.bfloat16)
        v3[0:n] = jnp.zeros((n, HD, HD), jnp.bfloat16)
        rcv[1] = jnp.zeros(rcv.shape[1:], jnp.bfloat16)

    @pl.when(jnp.logical_not(has_next))
    def _():
        k3[2 * n : 3 * n] = jnp.zeros((n, HD, HD), jnp.bfloat16)
        v3[2 * n : 3 * n] = jnp.zeros((n, HD, HD), jnp.bfloat16)
        rcv[0] = jnp.zeros(rcv.shape[1:], jnp.bfloat16)

    for a in range(2):
        in_own(a).wait()
        for dr in range(rows):
            for dc in range(cols):
                r = dr * cols + dc
                if r > 0:
                    in_copy(a, peer(r, 1), peer(r, -1)).wait_recv()
            chunk = lax.rem(my_row - dr + rows, rows)
            for side, send_if, _ in sides:
                @pl.when(send_if)
                def _(a=a, side=side, chunk=chunk):
                    halo_copy(a, side, chunk).start()

    for a in range(2):
        for side, _, recv_if in sides:
            @pl.when(recv_if)
            def _(a=a, side=side):
                for chunk in range(rows):
                    halo_copy(a, side, chunk).wait_recv()

    half = slots // 2
    scale = HD ** -0.5
    out_arrays = ((ot, o_out), (dqt, dq_out), (dkt, dk_out), (dvt, dv_out))

    def out_copy(a, target, source):
        tiles, out = out_arrays[a]
        return pltpu.make_async_remote_copy(
            src_ref=tiles.at[target],
            dst_ref=out.at[0, :, pl.ds(pl.multiple_of(source * HD, HD), HD)],
            send_sem=out_send.at[a, target],
            recv_sem=out_recv.at[a, source],
            device_id=(target, frame),
            device_id_type=MESH,
        )

    def out_own(a):
        tiles, out = out_arrays[a]
        return pltpu.make_async_copy(
            tiles.at[me],
            out.at[0, :, pl.ds(pl.multiple_of(me * HD, HD), HD)],
            out_local.at[a],
        )

    def pair_of(ref, i, jj):
        return jnp.concatenate([ref[ci[i, 2 * jj]], ref[ci[i, 2 * jj + 1]]], axis=0)

    def query_phases(i, logits):
        held = {}

        def scores():
            q = qh[i]
            gt[i] = gh[i].astype(jnp.float32).T.astype(jnp.bfloat16)
            qt[i] = q.astype(jnp.float32).T.astype(jnp.bfloat16)
            top = jnp.full((HD, HD), NEG, jnp.float32)
            for jj in range(half):
                s = dot_nt(q, pair_of(k3, i, jj)) * (scale * LOG2E)
                s0 = s[:, :HD] + bias[i, 2 * jj]
                s1 = s[:, HD:] + bias[i, 2 * jj + 1]
                logits[:, jj * 2 * HD : jj * 2 * HD + HD] = s0
                logits[:, jj * 2 * HD + HD : (jj + 1) * 2 * HD] = s1
                top = jnp.maximum(top, jnp.maximum(s0, s1))
                yield
            held["highest"] = jnp.max(top, axis=1, keepdims=True)

        def output():
            highest = held["highest"]
            total = jnp.zeros((HD, HD), jnp.float32)
            o = jnp.zeros((HD, HD), jnp.float32)
            for jj in range(half):
                at = slice(jj * 2 * HD, (jj + 1) * 2 * HD)
                p = jnp.exp2(logits[:, at] - highest)
                logits[:, at] = p
                total = total + (p[:, :HD] + p[:, HD:])
                o = o + dot_nn(p.astype(jnp.bfloat16), pair_of(v3, i, jj))
                yield
            inv = 1.0 / jnp.sum(total, axis=1, keepdims=True)
            ob = (o * inv).astype(jnp.bfloat16)
            ot[i] = ob
            held["inv"] = inv
            held["row_dot"] = jnp.sum(
                gh[i].astype(jnp.float32) * ob.astype(jnp.float32), axis=1, keepdims=True)

        def gradients():
            g, inv, row_dot = gh[i], held["inv"], held["row_dot"]
            dq = jnp.zeros((HD, HD), jnp.float32)
            for jj in range(half):
                at = slice(jj * 2 * HD, (jj + 1) * 2 * HD)
                p = logits[:, at] * inv
                dp = dot_nt(g, pair_of(v3, i, jj))
                ds = (p * (dp - row_dot)).astype(jnp.bfloat16)
                pb = p.astype(jnp.bfloat16)
                dq = dq + dot_nn(ds, pair_of(k3, i, jj))
                base = i * slots + 2 * jj
                pst[base] = pb[:, :HD]
                pst[base + 1] = pb[:, HD:]
                dst[base] = ds[:, :HD]
                dst[base + 1] = ds[:, HD:]
                yield
            dqt[i] = (dq * scale).astype(jnp.bfloat16)

        return scores, output, gradients

    def query_block(b, _):
        tiles = [peer(b * BLOCK + u, -1) for u in range(BLOCK)]
        for u in range(BLOCK):
            r = b * BLOCK + u

            def came(r=r, u=u):
                for a in (2, 3):
                    in_copy(a, peer(r, 1), tiles[u]).wait_recv()

            if u > 0:
                came()
            else:
                pl.when(b > 0)(came)

                @pl.when(b == 0)
                def _():
                    for a in (2, 3):
                        in_own(a).wait()

        steps = [query_phases(tiles[u], sbuf.at[u]) for u in range(BLOCK)]
        together(steps[0][0]())
        for u in range(BLOCK):
            if u + 1 < BLOCK:
                together(steps[u][1](), steps[u + 1][0]())
                together(steps[u][2]())
            else:
                together(steps[u][1]())
                together(steps[u][2]())
        for u in range(BLOCK):

            def leave(u=u):
                for a in (0, 1):
                    out_copy(a, tiles[u], me).start()

            if u > 0:
                leave()
            else:
                pl.when(b > 0)(leave)

                @pl.when(b == 0)
                def _():
                    for a in (0, 1):
                        out_own(a).start()
        return 0

    lax.fori_loop(0, n // BLOCK, query_block, 0)

    def key_side(a):
        left, right, par = ((qt, dst, park), (gt, pst, parv))[a]

        def group(x, acc):
            one, two = gp[2 * x], gp[2 * x + 1]
            term = dot_nn(
                jnp.concatenate([left[gq[2 * x]], left[gq[2 * x + 1]]], axis=1),
                jnp.concatenate([right[one], right[two]], axis=0))
            acc = acc * keep[x] + term
            par[x] = (acc * scale if a == 0 else acc).astype(jnp.bfloat16)
            return acc

        lax.fori_loop(0, groups, group, jnp.zeros((HD, HD), jnp.float32), unroll=12)

    def tile_of(a, t):
        return (park, parv)[a][last[t]].T

    def gr_copy(a, side, i):
        return pltpu.make_async_remote_copy(
            src_ref=snd.at[side, a, i],
            dst_ref=rcv.at[side, a, i],
            send_sem=gr_send.at[side, a, i],
            recv_sem=gr_recv.at[side, a, i],
            device_id=(me, frame - 1 if side == 0 else frame + 1),
            device_id_type=MESH,
        )

    def neighbour_terms(a):
        def four(b, _):
            for side, send_if, _ in sides:
                @pl.when(send_if)
                def _(side=side):
                    for u in range(BLOCK):
                        i = b * BLOCK + u
                        snd[side, a, i] = tile_of(a, i if side == 0 else 2 * n + i)
                    for u in range(BLOCK):
                        gr_copy(a, side, b * BLOCK + u).start()
            return 0

        lax.fori_loop(0, n // BLOCK, four, 0)

    def finish(a):
        def four(b, _):
            tiles = [peer(b * BLOCK + u, -1) for u in range(BLOCK)]
            for side, _, recv_if in sides:
                @pl.when(recv_if)
                def _(side=side):
                    for i in tiles:
                        gr_copy(a, side, i).wait_recv()
            for i in tiles:
                tot = tile_of(a, n + i).astype(jnp.float32)
                tot = tot + rcv[0, a, i].astype(jnp.float32) + rcv[1, a, i].astype(jnp.float32)
                (dkt, dvt)[a][i] = tot.astype(jnp.bfloat16)
            for u, i in enumerate(tiles):

                def leave(i=i):
                    out_copy(2 + a, i, me).start()

                if u > 0:
                    leave()
                else:
                    pl.when(b > 0)(leave)

                    @pl.when(b == 0)
                    def _():
                        out_own(2 + a).start()
            return 0

        lax.fori_loop(0, n // BLOCK, four, 0)

    key_side(1)
    neighbour_terms(1)
    key_side(0)
    neighbour_terms(0)
    finish(1)
    finish(0)

    for a in range(4):
        out_own(a).wait()

        def settle(r, _, a=a):
            there, back = peer(r, 1), peer(r, -1)
            in_copy(a, there, me).wait_send()
            out_copy(a, back, me).wait_send()
            out_copy(a, there, back).wait_recv()
            return 0

        lax.fori_loop(1, n, settle, 0)
    for side, send_if, _ in sides:
        @pl.when(send_if)
        def _(side=side):
            for a in range(2):
                for chunk in range(rows):
                    halo_copy(a, side, chunk).wait_send()

            def settle_terms(i, _):
                for a in range(2):
                    gr_copy(a, side, i).wait_send()
                return 0

            lax.fori_loop(0, n, settle_terms, 0)


def tables(window, slots, groups):
    n, total = window.shape
    w = window > 0
    t = jnp.arange(total, dtype=jnp.int32)
    i = jnp.arange(n, dtype=jnp.int32)
    before = (t[:, None] < t[None, :]).astype(jnp.int32)
    pos = jnp.sum(window[:, :, None] * before[None], axis=1)
    count = jnp.sum(window, axis=1)
    j = jnp.arange(slots, dtype=jnp.int32)
    hit = w[:, None, :] & (pos[:, None, :] == j[None, :, None])
    chosen = jnp.sum(jnp.where(hit, t[None, None, :], 0), axis=2)
    present = j[None, :] < count[:, None]
    chosen = jnp.where(present, chosen, n + i[:, None])
    bias = jnp.where(present, 0.0, NEG).astype(jnp.float32)
    pair = i[:, None] * slots + pos
    number = jnp.sum(window, axis=0)
    rank = jnp.sum(window[:, None, :] * (i[:, None, None] < i[None, :, None]).astype(jnp.int32), axis=0)
    used = (number + 1) // 2
    start = jnp.sum(used[:, None] * before, axis=0)
    place = jnp.where(w, 2 * start[None, :] + rank, -1)
    x = jnp.arange(2 * groups, dtype=jnp.int32)
    found = place.reshape(1, -1) == x[:, None]
    gp = jnp.sum(jnp.where(found, pair.reshape(1, -1) - n * slots, 0), axis=1) + n * slots
    gq = jnp.minimum(gp // slots, n - 1)
    opens = jnp.any((start[None, :] == jnp.arange(groups)[:, None]) & (number > 0)[None, :], axis=1)
    keep = jnp.where(opens, 0.0, 1.0).astype(jnp.float32)
    last = jnp.where(number > 0, start + used - 1, groups)
    return chosen, bias, gp, gq, keep, last


def body(shape, queries, keys, values, out_grad, tile_mask):
    rows, cols, frames = shape
    n = rows * cols
    slots = min(18, 3 * n)
    groups = (n * slots + 3 * n) // 2
    frame = lax.axis_index("ctx")
    padded = jnp.pad(tile_mask[0], ((0, 0), (0, 0), (n, n)))
    own = lax.dynamic_index_in_dim(padded, frame, 0, keepdims=False)
    window = lax.dynamic_slice_in_dim(own, frame * n, 3 * n, 1)
    lists = tables(window, slots, groups)
    smem = pl.BlockSpec(memory_space=pltpu.SMEM)
    any_ = pl.BlockSpec(memory_space=pl.ANY)
    tile = lambda *lead: pltpu.VMEM(lead + (HD, HD), jnp.bfloat16)
    dma = pltpu.SemaphoreType.DMA
    return pl.pallas_call(
        functools.partial(kernel, rows, cols, slots, groups, frames),
        out_shape=[jax.ShapeDtypeStruct(queries.shape, jnp.bfloat16)] * 4,
        in_specs=[smem] * 6 + [any_] * 4,
        out_specs=[any_] * 4,
        scratch_shapes=[
            tile(3 * n), tile(3 * n), tile(n), tile(n),
            pltpu.VMEM((BLOCK, HD, slots * HD), jnp.float32),
            tile(n * slots + 1), tile(n * slots + 1),
            tile(n), tile(n),
            tile(groups + 1), tile(groups + 1),
            tile(n), tile(n), tile(2, 2, n), tile(2, 2, n), tile(n), tile(n),
            dma((4, n)), dma((4, n)), dma((4,)),
            dma((2, 2, rows)), dma((2, 2, rows)),
            dma((2, 2, n)), dma((2, 2, n)),
            dma((4, n)), dma((4, n)), dma((4,)),
        ],
        compiler_params=pltpu.CompilerParams(
            collective_id=0, has_side_effects=True, vmem_limit_bytes=56 * 1024 * 1024),
    )(*lists, queries, keys, values, out_grad)


def solution(mesh):
    n, frames = mesh.shape["seq"], mesh.shape["ctx"]
    cols = 4 if n % 4 == 0 and n > 4 else 2
    shape = (n // cols, cols, frames)
    data = P("ctx", "seq", None)
    return jax.shard_map(
        functools.partial(body, shape),
        mesh=mesh,
        in_specs=(data,) * 4 + (P("seq", None, None, None),),
        out_specs=(data,) * 4,
        check_vma=False,
    )
```

```python
import functools

import jax
import jax.numpy as jnp
from jax import lax
from jax.experimental import pallas as pl
from jax.experimental.pallas import tpu as pltpu
from jax.sharding import PartitionSpec as P

MESH = pl.DeviceIdType.MESH
HD = 128
LOG2E = 1.4426950408889634
NEG = -1e30
BLOCK = 4


def dot_nt(a, b):
    return lax.dot_general(a, b, (((1,), (1,)), ((), ())), preferred_element_type=jnp.float32)


def dot_nn(a, b):
    return lax.dot_general(a, b, (((1,), (0,)), ((), ())), preferred_element_type=jnp.float32)


def together(*parts):
    parts = list(parts)
    while parts:
        for part in list(parts):
            if next(part, True):
                parts.remove(part)


def build_tables(mask, frame, slots, groups, tables):
    chosen, pairs, owners, last, bias, hold = tables
    n, total = mask.shape
    lines = pairs.shape[0]
    iota = lambda dims, at: lax.broadcasted_iota(jnp.int32, dims, at)
    flag = lambda x: jnp.where(x, 1.0, 0.0).astype(jnp.bfloat16)
    w = mask[...]
    wf = w.astype(jnp.float32)
    wb = wf.astype(jnp.bfloat16)
    before = flag(iota((total, total), 0) < iota((total, total), 1))
    pos = dot_nn(wb, before)
    count = jnp.sum(wf, axis=1, keepdims=True)
    lane = iota((n, HD), 1)
    tile = (iota((n, total), 1) - (frame - 1) * n).astype(jnp.float32)
    own = (n + iota((n, 1), 0)).astype(jnp.float32)
    row = jnp.zeros((n, HD), jnp.float32)
    for j in range(slots):
        here = jnp.sum(jnp.where((w > 0) & (pos == j), tile, 0.0), axis=1, keepdims=True)
        here = jnp.where(count > j, here, own)
        row = jnp.where(lane == j, here, row)
    chosen[...] = row.astype(jnp.int32)
    bias[...] = jnp.where(lane.astype(jnp.float32) < count, 0.0, NEG)
    rank = dot_nn(flag(iota((n, n), 0) > iota((n, n), 1)), wb)
    number = jnp.sum(w, axis=0, keepdims=True)
    used = lax.shift_right_logical(number + 1, 1)
    start = dot_nn(jnp.broadcast_to(used, (8, total)).astype(jnp.float32).astype(jnp.bfloat16), before)
    final = jnp.where(number > 0, start.astype(jnp.int32) + used - 1, groups)
    last[...] = final
    place = jnp.where(w > 0, (2.0 * start[0:1] + rank).astype(jnp.int32), -16)
    line, at = lax.shift_right_arithmetic(place, 4), place & 15
    opens = jnp.where(rank == 0, 1.0, 0.0)
    pair_of = jnp.full((lines, 16), n * slots, jnp.float32)
    owner_of = jnp.zeros((lines, 16), jnp.float32)
    opens_of = jnp.zeros((lines, 16), jnp.float32)
    for i in range(n):
        left = flag(iota((lines, total), 0) == line[i : i + 1])
        right = jnp.where(iota((16, total), 0) == at[i : i + 1], 1.0, 0.0)
        both = jnp.concatenate([right, right * pos[i : i + 1], right * opens[i : i + 1]], axis=0)
        found = dot_nt(left, both.astype(jnp.bfloat16))
        pair_of = pair_of + found[:, :16] * ((i - n) * slots) + found[:, 16:32]
        owner_of = owner_of + found[:, :16] * i
        opens_of = opens_of + found[:, 32:48]
    wide = lambda x: jnp.concatenate([x, jnp.zeros((lines, HD - 16), jnp.float32)], axis=1)
    pairs[...] = wide(pair_of).astype(jnp.int32)
    owners[...] = wide(owner_of).astype(jnp.int32)
    hold[...] = 1.0 - wide(opens_of)


def kernel(
    rows, cols, slots, groups, frames,
    q_in, k_in, v_in, g_in, mask_in,
    o_out, dq_out, dk_out, dv_out,
    k3, v3, qh, gh, sbuf, pst, dst, qt, gt, park, parv, ot, dqt, snd, rcv, dkt, dvt,
    mask, ci_v, gp_v, gq_v, last_v, bias_v, hold_v, ci, gp, gq, last, bias, hold, mask_sem, table_sem,
    in_send, in_recv, in_local, halo_send, halo_recv, gr_send, gr_recv, out_send, out_recv, out_local,
):
    n = rows * cols
    me = lax.axis_index("seq")
    frame = lax.axis_index("ctx")
    my_row, my_col = me // cols, me % cols
    has_prev, has_next = frame > 0, frame < frames - 1

    def peer(r, sign):
        dr, dc = r // cols, r % cols
        row = lax.rem(my_row + sign * dr + rows, rows)
        col = lax.rem(my_col + sign * dc + cols, cols)
        return row * cols + col

    mask_copy = pltpu.make_async_copy(mask_in.at[0, frame], mask, mask_sem)
    mask_copy.start()
    barrier = pltpu.get_barrier_semaphore()

    def greet(r, _):
        pl.semaphore_signal(barrier, inc=1, device_id=(peer(r, 1), frame), device_id_type=MESH)
        return 0

    lax.fori_loop(1, n, greet, 0)

    for step in (1, frames - 1):
        beside = lax.rem(frame + step, frames)
        pl.semaphore_signal(barrier, inc=1, device_id=(me, beside), device_id_type=MESH)
    pl.semaphore_wait(barrier, n + 1)

    arrays = ((k_in, k3, n), (v_in, v3, n), (q_in, qh, 0), (g_in, gh, 0))

    def in_copy(a, target, source):
        src, dst_ref, base = arrays[a]
        return pltpu.make_async_remote_copy(
            src_ref=src.at[0, :, pl.ds(pl.multiple_of(target * HD, HD), HD)],
            dst_ref=dst_ref.at[base + source],
            send_sem=in_send.at[a, target],
            recv_sem=in_recv.at[a, source],
            device_id=(target, frame),
            device_id_type=MESH,
        )

    def in_own(a):
        src, dst_ref, base = arrays[a]
        return pltpu.make_async_copy(
            src.at[0, :, pl.ds(pl.multiple_of(me * HD, HD), HD)],
            dst_ref.at[base + me],
            in_local.at[a],
        )

    for a in range(4):
        in_own(a).start()

        def send(r, _, a=a):
            in_copy(a, peer(r, 1), me).start()
            return 0

        lax.fori_loop(1, n, send, 0)

    def halo_copy(a, side, chunk):
        ref = (k3, v3)[a]
        first = chunk * cols
        return pltpu.make_async_remote_copy(
            src_ref=ref.at[pl.ds(n + first, cols)],
            dst_ref=ref.at[pl.ds((2 * n if side == 0 else 0) + first, cols)],
            send_sem=halo_send.at[a, side, chunk],
            recv_sem=halo_recv.at[a, side, chunk],
            device_id=(me, frame - 1 if side == 0 else frame + 1),
            device_id_type=MESH,
        )

    sides = ((0, has_prev, has_next), (1, has_next, has_prev))
    mask_copy.wait()
    build_tables(mask, frame, slots, groups, (ci_v, gp_v, gq_v, last_v, bias_v, hold_v))
    moves = [
        pltpu.make_async_copy(built, table, table_sem.at[at])
        for at, (built, table) in enumerate(
            zip((ci_v, gp_v, gq_v, last_v, bias_v, hold_v), (ci, gp, gq, last, bias, hold)))
    ]
    for move in moves:
        move.start()
    zero_tile = jnp.zeros((HD, HD), jnp.bfloat16)
    pst[n * slots] = zero_tile
    dst[n * slots] = zero_tile
    park[groups] = zero_tile
    parv[groups] = zero_tile

    @pl.when(jnp.logical_not(has_prev))
    def _():
        k3[0:n] = jnp.zeros((n, HD, HD), jnp.bfloat16)
        v3[0:n] = jnp.zeros((n, HD, HD), jnp.bfloat16)
        rcv[1] = jnp.zeros(rcv.shape[1:], jnp.bfloat16)

    @pl.when(jnp.logical_not(has_next))
    def _():
        k3[2 * n : 3 * n] = jnp.zeros((n, HD, HD), jnp.bfloat16)
        v3[2 * n : 3 * n] = jnp.zeros((n, HD, HD), jnp.bfloat16)
        rcv[0] = jnp.zeros(rcv.shape[1:], jnp.bfloat16)

    for move in moves:
        move.wait()

    for a in range(2):
        in_own(a).wait()
        for dr in range(rows):
            for dc in range(cols):
                r = dr * cols + dc
                if r > 0:
                    in_copy(a, peer(r, 1), peer(r, -1)).wait_recv()
            chunk = lax.rem(my_row - dr + rows, rows)
            for side, send_if, _ in sides:
                @pl.when(send_if)
                def _(a=a, side=side, chunk=chunk):
                    halo_copy(a, side, chunk).start()

    for a in range(2):
        for side, _, recv_if in sides:
            @pl.when(recv_if)
            def _(a=a, side=side):
                for chunk in range(rows):
                    halo_copy(a, side, chunk).wait_recv()

    half = slots // 2
    scale = HD ** -0.5
    out_arrays = ((ot, o_out), (dqt, dq_out), (dkt, dk_out), (dvt, dv_out))

    def out_copy(a, target, source):
        tiles, out = out_arrays[a]
        return pltpu.make_async_remote_copy(
            src_ref=tiles.at[target],
            dst_ref=out.at[0, :, pl.ds(pl.multiple_of(source * HD, HD), HD)],
            send_sem=out_send.at[a, target],
            recv_sem=out_recv.at[a, source],
            device_id=(target, frame),
            device_id_type=MESH,
        )

    def out_own(a):
        tiles, out = out_arrays[a]
        return pltpu.make_async_copy(
            tiles.at[me],
            out.at[0, :, pl.ds(pl.multiple_of(me * HD, HD), HD)],
            out_local.at[a],
        )

    def within(at, size):
        return jnp.minimum(jnp.maximum(at, 0), size - 1)

    def pair_of(ref, i, jj):
        one, two = within(ci[i, 2 * jj], 3 * n), within(ci[i, 2 * jj + 1], 3 * n)
        return jnp.concatenate([ref[one], ref[two]], axis=0)

    def query_phases(i, logits):
        held = {}

        def scores():
            q = qh[i]
            gt[i] = gh[i].astype(jnp.float32).T.astype(jnp.bfloat16)
            qt[i] = q.astype(jnp.float32).T.astype(jnp.bfloat16)
            top = jnp.full((HD, HD), NEG, jnp.float32)
            for jj in range(half):
                s = dot_nt(q, pair_of(k3, i, jj)) * (scale * LOG2E)
                s0 = s[:, :HD] + bias[i, 2 * jj]
                s1 = s[:, HD:] + bias[i, 2 * jj + 1]
                logits[:, jj * 2 * HD : jj * 2 * HD + HD] = s0
                logits[:, jj * 2 * HD + HD : (jj + 1) * 2 * HD] = s1
                top = jnp.maximum(top, jnp.maximum(s0, s1))
                yield
            held["highest"] = jnp.max(top, axis=1, keepdims=True)

        def output():
            highest = held["highest"]
            total = jnp.zeros((HD, HD), jnp.float32)
            o = jnp.zeros((HD, HD), jnp.float32)
            for jj in range(half):
                at = slice(jj * 2 * HD, (jj + 1) * 2 * HD)
                p = jnp.exp2(logits[:, at] - highest)
                logits[:, at] = p
                total = total + (p[:, :HD] + p[:, HD:])
                o = o + dot_nn(p.astype(jnp.bfloat16), pair_of(v3, i, jj))
                yield
            inv = 1.0 / jnp.sum(total, axis=1, keepdims=True)
            ob = (o * inv).astype(jnp.bfloat16)
            ot[i] = ob
            held["inv"] = inv
            held["row_dot"] = jnp.sum(
                gh[i].astype(jnp.float32) * ob.astype(jnp.float32), axis=1, keepdims=True)

        def gradients():
            g, inv, row_dot = gh[i], held["inv"], held["row_dot"]
            dq = jnp.zeros((HD, HD), jnp.float32)
            for jj in range(half):
                at = slice(jj * 2 * HD, (jj + 1) * 2 * HD)
                p = logits[:, at] * inv
                dp = dot_nt(g, pair_of(v3, i, jj))
                ds = (p * (dp - row_dot)).astype(jnp.bfloat16)
                pb = p.astype(jnp.bfloat16)
                dq = dq + dot_nn(ds, pair_of(k3, i, jj))
                base = i * slots + 2 * jj
                pst[base] = pb[:, :HD]
                pst[base + 1] = pb[:, HD:]
                dst[base] = ds[:, :HD]
                dst[base + 1] = ds[:, HD:]
                yield
            dqt[i] = (dq * scale).astype(jnp.bfloat16)

        return scores, output, gradients

    def query_block(b, _):
        tiles = [peer(b * BLOCK + u, -1) for u in range(BLOCK)]
        for u in range(BLOCK):
            r = b * BLOCK + u

            def came(r=r, u=u):
                for a in (2, 3):
                    in_copy(a, peer(r, 1), tiles[u]).wait_recv()

            if u > 0:
                came()
            else:
                pl.when(b > 0)(came)

                @pl.when(b == 0)
                def _():
                    for a in (2, 3):
                        in_own(a).wait()

        steps = [query_phases(tiles[u], sbuf.at[u]) for u in range(BLOCK)]
        together(steps[0][0]())
        for u in range(BLOCK):
            if u + 1 < BLOCK:
                together(steps[u][1](), steps[u + 1][0]())
                together(steps[u][2]())
            else:
                together(steps[u][1]())
                together(steps[u][2]())
        for u in range(BLOCK):

            def leave(u=u):
                for a in (0, 1):
                    out_copy(a, tiles[u], me).start()

            if u > 0:
                leave()
            else:
                pl.when(b > 0)(leave)

                @pl.when(b == 0)
                def _():
                    for a in (0, 1):
                        out_own(a).start()
        return 0

    lax.fori_loop(0, n // BLOCK, query_block, 0)

    def key_side(a):
        left, right, par = ((qt, dst, park), (gt, pst, parv))[a]

        def row(y, acc):
            for u in range(8):
                whose = [within(gq[y, 2 * u + k], n) for k in range(2)]
                which = [within(gp[y, 2 * u + k], n * slots + 1) for k in range(2)]
                term = dot_nn(
                    jnp.concatenate([left[k] for k in whose], axis=1),
                    jnp.concatenate([right[k] for k in which], axis=0))
                acc = acc * hold[y, 2 * u] + term
                par[8 * y + u] = (acc * scale if a == 0 else acc).astype(jnp.bfloat16)
            return acc

        lines = groups // 8
        unroll = 3 if lines % 3 == 0 else 1
        lax.fori_loop(0, lines, row, jnp.zeros((HD, HD), jnp.float32), unroll=unroll)

    def tile_of(a, t):
        return (park, parv)[a][within(last[0, (frame - 1) * n + t], groups + 1)].T

    def gr_copy(a, side, i):
        return pltpu.make_async_remote_copy(
            src_ref=snd.at[side, a, i],
            dst_ref=rcv.at[side, a, i],
            send_sem=gr_send.at[side, a, i],
            recv_sem=gr_recv.at[side, a, i],
            device_id=(me, frame - 1 if side == 0 else frame + 1),
            device_id_type=MESH,
        )

    def neighbour_terms(a):
        def four(b, _):
            for side, send_if, _ in sides:
                @pl.when(send_if)
                def _(side=side):
                    for u in range(BLOCK):
                        i = b * BLOCK + u
                        snd[side, a, i] = tile_of(a, i if side == 0 else 2 * n + i)
                    for u in range(BLOCK):
                        gr_copy(a, side, b * BLOCK + u).start()
            return 0

        lax.fori_loop(0, n // BLOCK, four, 0)

    def finish(a):
        def four(b, _):
            tiles = [peer(b * BLOCK + u, -1) for u in range(BLOCK)]
            for side, _, recv_if in sides:
                @pl.when(recv_if)
                def _(side=side):
                    for i in tiles:
                        gr_copy(a, side, i).wait_recv()
            for i in tiles:
                tot = tile_of(a, n + i).astype(jnp.float32)
                tot = tot + rcv[0, a, i].astype(jnp.float32) + rcv[1, a, i].astype(jnp.float32)
                (dkt, dvt)[a][i] = tot.astype(jnp.bfloat16)
            for u, i in enumerate(tiles):

                def leave(i=i):
                    out_copy(2 + a, i, me).start()

                if u > 0:
                    leave()
                else:
                    pl.when(b > 0)(leave)

                    @pl.when(b == 0)
                    def _():
                        out_own(2 + a).start()
            return 0

        lax.fori_loop(0, n // BLOCK, four, 0)

    key_side(1)
    neighbour_terms(1)
    key_side(0)
    neighbour_terms(0)
    finish(1)
    finish(0)

    for a in range(4):
        out_own(a).wait()

        def settle(r, _, a=a):
            there, back = peer(r, 1), peer(r, -1)
            in_copy(a, there, me).wait_send()
            out_copy(a, back, me).wait_send()
            out_copy(a, there, back).wait_recv()
            return 0

        lax.fori_loop(1, n, settle, 0)
    for side, send_if, _ in sides:
        @pl.when(send_if)
        def _(side=side):
            for a in range(2):
                for chunk in range(rows):
                    halo_copy(a, side, chunk).wait_send()

            def settle_terms(i, _):
                for a in range(2):
                    gr_copy(a, side, i).wait_send()
                return 0

            lax.fori_loop(0, n, settle_terms, 0)


def body(shape, queries, keys, values, out_grad, tile_mask):
    rows, cols, frames = shape
    n = rows * cols
    slots = min(18, 3 * n)
    groups = -(-(n * slots + 3 * n) // 16) * 8
    lines = -(-groups // 256) * 32
    any_ = pl.BlockSpec(memory_space=pl.ANY)
    tile = lambda *lead: pltpu.VMEM(lead + (HD, HD), jnp.bfloat16)
    dma = pltpu.SemaphoreType.DMA
    table_shapes = (
        ((n, HD), jnp.int32), ((lines, HD), jnp.int32), ((lines, HD), jnp.int32),
        ((8, frames * n), jnp.int32), ((n, HD), jnp.float32), ((lines, HD), jnp.float32))
    return pl.pallas_call(
        functools.partial(kernel, rows, cols, slots, groups, frames),
        out_shape=[jax.ShapeDtypeStruct(queries.shape, jnp.bfloat16)] * 4,
        in_specs=[any_] * 5,
        out_specs=[any_] * 4,
        scratch_shapes=[
            tile(3 * n), tile(3 * n), tile(n), tile(n),
            pltpu.VMEM((BLOCK, HD, slots * HD), jnp.float32),
            tile(n * slots + 1), tile(n * slots + 1),
            tile(n), tile(n),
            tile(groups + 1), tile(groups + 1),
            tile(n), tile(n), tile(2, 2, n), tile(2, 2, n), tile(n), tile(n),
            pltpu.VMEM((n, frames * n), jnp.int32),
            *[pltpu.VMEM(dims, kind) for dims, kind in table_shapes],
            *[pltpu.SMEM(dims, kind) for dims, kind in table_shapes],
            dma, dma((6,)),
            dma((4, n)), dma((4, n)), dma((4,)),
            dma((2, 2, rows)), dma((2, 2, rows)),
            dma((2, 2, n)), dma((2, 2, n)),
            dma((4, n)), dma((4, n)), dma((4,)),
        ],
        compiler_params=pltpu.CompilerParams(
            collective_id=0, has_side_effects=True, vmem_limit_bytes=56 * 1024 * 1024),
    )(queries, keys, values, out_grad, tile_mask)


def solution(mesh):
    n, frames = mesh.shape["seq"], mesh.shape["ctx"]
    cols = 4 if n % 4 == 0 and n > 4 else 2
    shape = (n // cols, cols, frames)
    data = P("ctx", "seq", None)
    return jax.shard_map(
        functools.partial(body, shape),
        mesh=mesh,
        in_specs=(data,) * 4 + (P("seq", None, None, None),),
        out_specs=(data,) * 4,
        check_vma=False,
    )
```

```python
import functools

import jax
import jax.numpy as jnp
from jax import lax
from jax.experimental import pallas as pl
from jax.experimental.pallas import tpu as pltpu
from jax.sharding import PartitionSpec as P

MESH = pl.DeviceIdType.MESH
HD = 128
LOG2E = 1.4426950408889634
NEG = -1e30
BLOCK = 4


def dot_nt(a, b):
    return lax.dot_general(a, b, (((1,), (1,)), ((), ())), preferred_element_type=jnp.float32)


def dot_nn(a, b):
    return lax.dot_general(a, b, (((1,), (0,)), ((), ())), preferred_element_type=jnp.float32)


def together(*parts):
    parts = list(parts)
    while parts:
        for part in list(parts):
            if next(part, True):
                parts.remove(part)


def build_tables(mask, frame, slots, groups, tables):
    chosen, pairs, owners, last, bias, hold = tables
    n, total = mask.shape
    lines = pairs.shape[0]
    iota = lambda dims, at: lax.broadcasted_iota(jnp.int32, dims, at)
    flag = lambda x: jnp.where(x, 1.0, 0.0).astype(jnp.bfloat16)
    w = mask[...]
    wf = w.astype(jnp.float32)
    wb = wf.astype(jnp.bfloat16)
    before = flag(iota((total, total), 0) < iota((total, total), 1))
    pos = dot_nn(wb, before)
    count = jnp.sum(wf, axis=1, keepdims=True)
    lane = iota((n, HD), 1)
    tile = (iota((n, total), 1) - (frame - 1) * n).astype(jnp.float32)
    own = (n + iota((n, 1), 0)).astype(jnp.float32)
    row = jnp.zeros((n, HD), jnp.float32)
    for j in range(slots):
        here = jnp.sum(jnp.where((w > 0) & (pos == j), tile, 0.0), axis=1, keepdims=True)
        here = jnp.where(count > j, here, own)
        row = jnp.where(lane == j, here, row)
    chosen[...] = row.astype(jnp.int32)
    bias[...] = jnp.where(lane.astype(jnp.float32) < count, 0.0, NEG)
    rank = dot_nn(flag(iota((n, n), 0) > iota((n, n), 1)), wb)
    number = jnp.sum(w, axis=0, keepdims=True)
    used = lax.shift_right_logical(number + 1, 1)
    start = dot_nn(jnp.broadcast_to(used, (8, total)).astype(jnp.float32).astype(jnp.bfloat16), before)
    final = jnp.where(number > 0, start.astype(jnp.int32) + used - 1, groups)
    last[...] = final
    place = jnp.where(w > 0, (2.0 * start[0:1] + rank).astype(jnp.int32), -16)
    line, at = lax.shift_right_arithmetic(place, 4), place & 15
    opens = jnp.where(rank == 0, 1.0, 0.0)
    pair_of = jnp.full((lines, 16), n * slots, jnp.float32)
    owner_of = jnp.zeros((lines, 16), jnp.float32)
    opens_of = jnp.zeros((lines, 16), jnp.float32)
    for i in range(n):
        left = flag(iota((lines, total), 0) == line[i : i + 1])
        right = jnp.where(iota((16, total), 0) == at[i : i + 1], 1.0, 0.0)
        both = jnp.concatenate([right, right * pos[i : i + 1], right * opens[i : i + 1]], axis=0)
        found = dot_nt(left, both.astype(jnp.bfloat16))
        pair_of = pair_of + found[:, :16] * ((i - n) * slots) + found[:, 16:32]
        owner_of = owner_of + found[:, :16] * i
        opens_of = opens_of + found[:, 32:48]
    wide = lambda x: jnp.concatenate([x, jnp.zeros((lines, HD - 16), jnp.float32)], axis=1)
    pairs[...] = wide(pair_of).astype(jnp.int32)
    owners[...] = wide(owner_of).astype(jnp.int32)
    hold[...] = 1.0 - wide(opens_of)


def kernel(
    rows, cols, slots, groups, frames,
    q_in, k_in, v_in, g_in, mask_in,
    o_out, dq_out, dk_out, dv_out,
    k3, v3, qh, gh, sbuf, pst, dst, qt, gt, park, parv, ot, dqt, snd, rcv, dkt, dvt,
    mask, ci_v, gp_v, gq_v, last_v, bias_v, hold_v, ci, gp, gq, last, bias, hold, mask_sem, table_sem,
    in_send, in_recv, in_local, halo_send, halo_recv, gr_send, gr_recv, out_send, out_recv, out_local,
):
    n = rows * cols
    me = lax.axis_index("seq")
    frame = lax.axis_index("ctx")
    my_row, my_col = me // cols, me % cols
    has_prev, has_next = frame > 0, frame < frames - 1

    def peer(r, sign):
        dr, dc = r // cols, r % cols
        row = lax.rem(my_row + sign * dr + rows, rows)
        col = lax.rem(my_col + sign * dc + cols, cols)
        return row * cols + col

    mask_copy = pltpu.make_async_copy(mask_in.at[0, frame], mask, mask_sem)
    mask_copy.start()
    barrier = pltpu.get_barrier_semaphore()

    def greet(r, _):
        pl.semaphore_signal(barrier, inc=1, device_id=(peer(r, 1), frame), device_id_type=MESH)
        return 0

    lax.fori_loop(1, n, greet, 0)

    for step in (1, frames - 1):
        beside = lax.rem(frame + step, frames)
        pl.semaphore_signal(barrier, inc=1, device_id=(me, beside), device_id_type=MESH)
    pl.semaphore_wait(barrier, n + 1)

    arrays = ((k_in, k3, n), (v_in, v3, n), (q_in, qh, 0), (g_in, gh, 0))

    def in_copy(a, target, source):
        src, dst_ref, base = arrays[a]
        return pltpu.make_async_remote_copy(
            src_ref=src.at[0, :, pl.ds(pl.multiple_of(target * HD, HD), HD)],
            dst_ref=dst_ref.at[base + source],
            send_sem=in_send.at[a, target],
            recv_sem=in_recv.at[a, source],
            device_id=(target, frame),
            device_id_type=MESH,
        )

    def in_own(a):
        src, dst_ref, base = arrays[a]
        return pltpu.make_async_copy(
            src.at[0, :, pl.ds(pl.multiple_of(me * HD, HD), HD)],
            dst_ref.at[base + me],
            in_local.at[a],
        )

    for a in range(4):
        in_own(a).start()

    def send(first, last, a):
        def one(r, _):
            in_copy(a, peer(r, 1), me).start()
            return 0

        lax.fori_loop(first, last, one, 0)

    send(1, n, 0)
    send(1, n, 1)
    for dr in range(rows):
        for a in (2, 3):
            send(max(1, dr * cols), (dr + 1) * cols, a)

    def halo_copy(a, side, chunk):
        ref = (k3, v3)[a]
        first = chunk * cols
        return pltpu.make_async_remote_copy(
            src_ref=ref.at[pl.ds(n + first, cols)],
            dst_ref=ref.at[pl.ds((2 * n if side == 0 else 0) + first, cols)],
            send_sem=halo_send.at[a, side, chunk],
            recv_sem=halo_recv.at[a, side, chunk],
            device_id=(me, frame - 1 if side == 0 else frame + 1),
            device_id_type=MESH,
        )

    sides = ((0, has_prev, has_next), (1, has_next, has_prev))
    mask_copy.wait()
    build_tables(mask, frame, slots, groups, (ci_v, gp_v, gq_v, last_v, bias_v, hold_v))
    moves = [
        pltpu.make_async_copy(built, table, table_sem.at[at])
        for at, (built, table) in enumerate(
            zip((ci_v, gp_v, gq_v, last_v, bias_v, hold_v), (ci, gp, gq, last, bias, hold)))
    ]
    for move in moves:
        move.start()
    zero_tile = jnp.zeros((HD, HD), jnp.bfloat16)
    pst[n * slots] = zero_tile
    dst[n * slots] = zero_tile
    park[groups] = zero_tile
    parv[groups] = zero_tile

    @pl.when(jnp.logical_not(has_prev))
    def _():
        k3[0:n] = jnp.zeros((n, HD, HD), jnp.bfloat16)
        v3[0:n] = jnp.zeros((n, HD, HD), jnp.bfloat16)
        rcv[1] = jnp.zeros(rcv.shape[1:], jnp.bfloat16)

    @pl.when(jnp.logical_not(has_next))
    def _():
        k3[2 * n : 3 * n] = jnp.zeros((n, HD, HD), jnp.bfloat16)
        v3[2 * n : 3 * n] = jnp.zeros((n, HD, HD), jnp.bfloat16)
        rcv[0] = jnp.zeros(rcv.shape[1:], jnp.bfloat16)

    for move in moves:
        move.wait()

    for a in range(2):
        in_own(a).wait()
        for dr in range(rows):
            for dc in range(cols):
                r = dr * cols + dc
                if r > 0:
                    in_copy(a, peer(r, 1), peer(r, -1)).wait_recv()
            chunk = lax.rem(my_row - dr + rows, rows)
            for side, send_if, _ in sides:
                @pl.when(send_if)
                def _(a=a, side=side, chunk=chunk):
                    halo_copy(a, side, chunk).start()

    for a in range(2):
        for side, _, recv_if in sides:
            @pl.when(recv_if)
            def _(a=a, side=side):
                for chunk in range(rows):
                    halo_copy(a, side, chunk).wait_recv()

    half = slots // 2
    scale = HD ** -0.5
    out_arrays = ((ot, o_out), (dqt, dq_out), (dkt, dk_out), (dvt, dv_out))

    def out_copy(a, target, source):
        tiles, out = out_arrays[a]
        return pltpu.make_async_remote_copy(
            src_ref=tiles.at[target],
            dst_ref=out.at[0, :, pl.ds(pl.multiple_of(source * HD, HD), HD)],
            send_sem=out_send.at[a, target],
            recv_sem=out_recv.at[a, source],
            device_id=(target, frame),
            device_id_type=MESH,
        )

    def out_own(a):
        tiles, out = out_arrays[a]
        return pltpu.make_async_copy(
            tiles.at[me],
            out.at[0, :, pl.ds(pl.multiple_of(me * HD, HD), HD)],
            out_local.at[a],
        )

    def within(at, size):
        return jnp.minimum(jnp.maximum(at, 0), size - 1)

    def pair_of(ref, i, jj):
        one, two = within(ci[i, 2 * jj], 3 * n), within(ci[i, 2 * jj + 1], 3 * n)
        return jnp.concatenate([ref[one], ref[two]], axis=0)

    def query_phases(i, logits):
        held = {}

        def scores():
            q = qh[i]
            gt[i] = gh[i].astype(jnp.float32).T.astype(jnp.bfloat16)
            qt[i] = q.astype(jnp.float32).T.astype(jnp.bfloat16)
            top = jnp.full((HD, HD), NEG, jnp.float32)
            for jj in range(half):
                s = dot_nt(q, pair_of(k3, i, jj)) * (scale * LOG2E)
                s0 = s[:, :HD] + bias[i, 2 * jj]
                s1 = s[:, HD:] + bias[i, 2 * jj + 1]
                logits[:, jj * 2 * HD : jj * 2 * HD + HD] = s0
                logits[:, jj * 2 * HD + HD : (jj + 1) * 2 * HD] = s1
                top = jnp.maximum(top, jnp.maximum(s0, s1))
                yield
            held["highest"] = jnp.max(top, axis=1, keepdims=True)

        def output():
            highest = held["highest"]
            total = jnp.zeros((HD, HD), jnp.float32)
            o = jnp.zeros((HD, HD), jnp.float32)
            for jj in range(half):
                at = slice(jj * 2 * HD, (jj + 1) * 2 * HD)
                p = jnp.exp2(logits[:, at] - highest)
                logits[:, at] = p
                total = total + (p[:, :HD] + p[:, HD:])
                o = o + dot_nn(p.astype(jnp.bfloat16), pair_of(v3, i, jj))
                yield
            inv = 1.0 / jnp.sum(total, axis=1, keepdims=True)
            ob = (o * inv).astype(jnp.bfloat16)
            ot[i] = ob
            held["inv"] = inv
            held["row_dot"] = jnp.sum(
                gh[i].astype(jnp.float32) * ob.astype(jnp.float32), axis=1, keepdims=True)

        def gradients():
            g, inv, row_dot = gh[i], held["inv"], held["row_dot"]
            dq = jnp.zeros((HD, HD), jnp.float32)
            for jj in range(half):
                at = slice(jj * 2 * HD, (jj + 1) * 2 * HD)
                p = logits[:, at] * inv
                dp = dot_nt(g, pair_of(v3, i, jj))
                ds = (p * (dp - row_dot)).astype(jnp.bfloat16)
                pb = p.astype(jnp.bfloat16)
                dq = dq + dot_nn(ds, pair_of(k3, i, jj))
                base = i * slots + 2 * jj
                pst[base] = pb[:, :HD]
                pst[base + 1] = pb[:, HD:]
                dst[base] = ds[:, :HD]
                dst[base + 1] = ds[:, HD:]
                yield
            dqt[i] = (dq * scale).astype(jnp.bfloat16)

        return scores, output, gradients

    def query_block(b, _):
        tiles = [peer(b * BLOCK + u, -1) for u in range(BLOCK)]
        for u in range(BLOCK):
            r = b * BLOCK + u

            def came(r=r, u=u):
                for a in (2, 3):
                    in_copy(a, peer(r, 1), tiles[u]).wait_recv()

            if u > 0:
                came()
            else:
                pl.when(b > 0)(came)

                @pl.when(b == 0)
                def _():
                    for a in (2, 3):
                        in_own(a).wait()

        steps = [query_phases(tiles[u], sbuf.at[u]) for u in range(BLOCK)]
        together(steps[0][0]())
        for u in range(BLOCK):
            if u + 1 < BLOCK:
                together(steps[u][1](), steps[u + 1][0]())
                together(steps[u][2]())
            else:
                together(steps[u][1]())
                together(steps[u][2]())
        for u in range(BLOCK):

            def leave(u=u):
                for a in (0, 1):
                    out_copy(a, tiles[u], me).start()

            if u > 0:
                leave()
            else:
                pl.when(b > 0)(leave)

                @pl.when(b == 0)
                def _():
                    for a in (0, 1):
                        out_own(a).start()
        return 0

    lax.fori_loop(0, n // BLOCK, query_block, 0)

    def key_side(a):
        left, right, par = ((qt, dst, park), (gt, pst, parv))[a]

        def row(y, acc):
            for u in range(8):
                whose = [within(gq[y, 2 * u + k], n) for k in range(2)]
                which = [within(gp[y, 2 * u + k], n * slots + 1) for k in range(2)]
                term = dot_nn(
                    jnp.concatenate([left[k] for k in whose], axis=1),
                    jnp.concatenate([right[k] for k in which], axis=0))
                acc = acc * hold[y, 2 * u] + term
                par[8 * y + u] = (acc * scale if a == 0 else acc).astype(jnp.bfloat16)
            return acc

        lines = groups // 8
        unroll = 3 if lines % 3 == 0 else 1
        lax.fori_loop(0, lines, row, jnp.zeros((HD, HD), jnp.float32), unroll=unroll)

    def tile_of(a, t):
        return (park, parv)[a][within(last[0, (frame - 1) * n + t], groups + 1)].T

    def gr_copy(a, side, i):
        return pltpu.make_async_remote_copy(
            src_ref=snd.at[side, a, i],
            dst_ref=rcv.at[side, a, i],
            send_sem=gr_send.at[side, a, i],
            recv_sem=gr_recv.at[side, a, i],
            device_id=(me, frame - 1 if side == 0 else frame + 1),
            device_id_type=MESH,
        )

    def neighbour_terms(a):
        def four(b, _):
            tiles = [peer(b * BLOCK + u, -1) for u in range(BLOCK)]
            for side, send_if, _ in sides:
                @pl.when(send_if)
                def _(side=side):
                    for i in tiles:
                        snd[side, a, i] = tile_of(a, i if side == 0 else 2 * n + i)
                    for i in tiles:
                        gr_copy(a, side, i).start()
            return 0

        lax.fori_loop(0, n // BLOCK, four, 0)

    def finish(a):
        def four(b, _):
            tiles = [peer(b * BLOCK + u, -1) for u in range(BLOCK)]
            for side, _, recv_if in sides:
                @pl.when(recv_if)
                def _(side=side):
                    for i in tiles:
                        gr_copy(a, side, i).wait_recv()
            for i in tiles:
                tot = tile_of(a, n + i).astype(jnp.float32)
                tot = tot + rcv[0, a, i].astype(jnp.float32) + rcv[1, a, i].astype(jnp.float32)
                (dkt, dvt)[a][i] = tot.astype(jnp.bfloat16)
            for u, i in enumerate(tiles):

                def leave(i=i):
                    out_copy(2 + a, i, me).start()

                if u > 0:
                    leave()
                else:
                    pl.when(b > 0)(leave)

                    @pl.when(b == 0)
                    def _():
                        out_own(2 + a).start()
            return 0

        lax.fori_loop(0, n // BLOCK, four, 0)

    key_side(1)
    neighbour_terms(1)
    key_side(0)
    neighbour_terms(0)
    finish(1)
    finish(0)

    for a in range(4):
        out_own(a).wait()

        def settle(r, _, a=a):
            there, back = peer(r, 1), peer(r, -1)
            in_copy(a, there, me).wait_send()
            out_copy(a, back, me).wait_send()
            out_copy(a, there, back).wait_recv()
            return 0

        lax.fori_loop(1, n, settle, 0)
    for side, send_if, _ in sides:
        @pl.when(send_if)
        def _(side=side):
            for a in range(2):
                for chunk in range(rows):
                    halo_copy(a, side, chunk).wait_send()

            def settle_terms(i, _):
                for a in range(2):
                    gr_copy(a, side, i).wait_send()
                return 0

            lax.fori_loop(0, n, settle_terms, 0)


def body(shape, queries, keys, values, out_grad, tile_mask):
    rows, cols, frames = shape
    n = rows * cols
    slots = min(18, 3 * n)
    groups = -(-(n * slots + 3 * n) // 16) * 8
    lines = -(-groups // 256) * 32
    any_ = pl.BlockSpec(memory_space=pl.ANY)
    tile = lambda *lead: pltpu.VMEM(lead + (HD, HD), jnp.bfloat16)
    dma = pltpu.SemaphoreType.DMA
    table_shapes = (
        ((n, HD), jnp.int32), ((lines, HD), jnp.int32), ((lines, HD), jnp.int32),
        ((8, frames * n), jnp.int32), ((n, HD), jnp.float32), ((lines, HD), jnp.float32))
    return pl.pallas_call(
        functools.partial(kernel, rows, cols, slots, groups, frames),
        out_shape=[jax.ShapeDtypeStruct(queries.shape, jnp.bfloat16)] * 4,
        in_specs=[any_] * 5,
        out_specs=[any_] * 4,
        scratch_shapes=[
            tile(3 * n), tile(3 * n), tile(n), tile(n),
            pltpu.VMEM((BLOCK, HD, slots * HD), jnp.float32),
            tile(n * slots + 1), tile(n * slots + 1),
            tile(n), tile(n),
            tile(groups + 1), tile(groups + 1),
            tile(n), tile(n), tile(2, 2, n), tile(2, 2, n), tile(n), tile(n),
            pltpu.VMEM((n, frames * n), jnp.int32),
            *[pltpu.VMEM(dims, kind) for dims, kind in table_shapes],
            *[pltpu.SMEM(dims, kind) for dims, kind in table_shapes],
            dma, dma((6,)),
            dma((4, n)), dma((4, n)), dma((4,)),
            dma((2, 2, rows)), dma((2, 2, rows)),
            dma((2, 2, n)), dma((2, 2, n)),
            dma((4, n)), dma((4, n)), dma((4,)),
        ],
        compiler_params=pltpu.CompilerParams(
            collective_id=0, has_side_effects=True, vmem_limit_bytes=56 * 1024 * 1024),
    )(queries, keys, values, out_grad, tile_mask)


def solution(mesh):
    n, frames = mesh.shape["seq"], mesh.shape["ctx"]
    cols = 4 if n % 4 == 0 and n > 4 else 2
    shape = (n // cols, cols, frames)
    data = P("ctx", "seq", None)
    return jax.shard_map(
        functools.partial(body, shape),
        mesh=mesh,
        in_specs=(data,) * 4 + (P("seq", None, None, None),),
        out_specs=(data,) * 4,
        check_vma=False,
    )
```

```python
import functools

import jax
import jax.numpy as jnp
from jax import lax
from jax.experimental import pallas as pl
from jax.experimental.pallas import tpu as pltpu
from jax.sharding import PartitionSpec as P

MESH = pl.DeviceIdType.MESH
HD = 128
LOG2E = 1.4426950408889634
NEG = -1e30
BLOCK = 4


def dot_nt(a, b):
    return lax.dot_general(a, b, (((1,), (1,)), ((), ())), preferred_element_type=jnp.float32)


def dot_nn(a, b):
    return lax.dot_general(a, b, (((1,), (0,)), ((), ())), preferred_element_type=jnp.float32)


def together(*parts):
    parts = list(parts)
    while parts:
        for part in list(parts):
            if next(part, True):
                parts.remove(part)


def build_tables(mask, frame, slots, groups, tables):
    chosen, pairs, owners, last, bias, hold = tables
    n, total = mask.shape
    lines = pairs.shape[0]
    iota = lambda dims, at: lax.broadcasted_iota(jnp.int32, dims, at)
    flag = lambda x: jnp.where(x, 1.0, 0.0).astype(jnp.bfloat16)
    w = mask[...]
    wf = w.astype(jnp.float32)
    wb = wf.astype(jnp.bfloat16)
    before = flag(iota((total, total), 0) < iota((total, total), 1))
    pos = dot_nn(wb, before)
    count = jnp.sum(wf, axis=1, keepdims=True)
    lane = iota((n, HD), 1)
    tile = (iota((n, total), 1) - (frame - 1) * n).astype(jnp.float32)
    own = (n + iota((n, 1), 0)).astype(jnp.float32)
    row = jnp.zeros((n, HD), jnp.float32)
    for j in range(slots):
        here = jnp.sum(jnp.where((w > 0) & (pos == j), tile, 0.0), axis=1, keepdims=True)
        here = jnp.where(count > j, here, own)
        row = jnp.where(lane == j, here, row)
    chosen[...] = row.astype(jnp.int32)
    bias[...] = jnp.where(lane.astype(jnp.float32) < count, 0.0, NEG)
    rank = dot_nn(flag(iota((n, n), 0) > iota((n, n), 1)), wb)
    number = jnp.sum(w, axis=0, keepdims=True)
    used = lax.shift_right_logical(number + 1, 1)
    start = dot_nn(jnp.broadcast_to(used, (8, total)).astype(jnp.float32).astype(jnp.bfloat16), before)
    final = jnp.where(number > 0, start.astype(jnp.int32) + used - 1, groups)
    last[...] = final
    place = jnp.where(w > 0, (2.0 * start[0:1] + rank).astype(jnp.int32), -16)
    line, at = lax.shift_right_arithmetic(place, 4), place & 15
    opens = jnp.where(rank == 0, 1.0, 0.0)
    pair_of = jnp.full((lines, 16), n * slots, jnp.float32)
    owner_of = jnp.zeros((lines, 16), jnp.float32)
    opens_of = jnp.zeros((lines, 16), jnp.float32)
    for i in range(n):
        left = flag(iota((lines, total), 0) == line[i : i + 1])
        right = jnp.where(iota((16, total), 0) == at[i : i + 1], 1.0, 0.0)
        both = jnp.concatenate([right, right * pos[i : i + 1], right * opens[i : i + 1]], axis=0)
        found = dot_nt(left, both.astype(jnp.bfloat16))
        pair_of = pair_of + found[:, :16] * ((i - n) * slots) + found[:, 16:32]
        owner_of = owner_of + found[:, :16] * i
        opens_of = opens_of + found[:, 32:48]
    wide = lambda x: jnp.concatenate([x, jnp.zeros((lines, HD - 16), jnp.float32)], axis=1)
    pairs[...] = wide(pair_of).astype(jnp.int32)
    owners[...] = wide(owner_of).astype(jnp.int32)
    hold[...] = 1.0 - wide(opens_of)


def kernel(
    rows, cols, slots, groups, frames,
    q_in, k_in, v_in, g_in, mask_in,
    o_out, dq_out, dk_out, dv_out,
    k3, v3, qh, gh, sbuf, row_dots, inverses, pst, dst, qt, gt, park, parv, ot, dqt, snd, rcv, dkt, dvt,
    mask, ci_v, gp_v, gq_v, last_v, bias_v, hold_v, ci, gp, gq, last, bias, hold, mask_sem, table_sem,
    in_send, in_recv, in_local, halo_send, halo_recv, gr_send, gr_recv, out_send, out_recv, out_local,
):
    n = rows * cols
    me = lax.axis_index("seq")
    frame = lax.axis_index("ctx")
    my_row, my_col = me // cols, me % cols
    has_prev, has_next = frame > 0, frame < frames - 1

    def peer(r, sign):
        dr, dc = r // cols, r % cols
        row = lax.rem(my_row + sign * dr + rows, rows)
        col = lax.rem(my_col + sign * dc + cols, cols)
        return row * cols + col

    mask_copy = pltpu.make_async_copy(mask_in.at[0, frame], mask, mask_sem)
    mask_copy.start()
    barrier = pltpu.get_barrier_semaphore()

    def greet(r, _):
        pl.semaphore_signal(barrier, inc=1, device_id=(peer(r, 1), frame), device_id_type=MESH)
        return 0

    lax.fori_loop(1, n, greet, 0)

    for step in (1, frames - 1):
        beside = lax.rem(frame + step, frames)
        pl.semaphore_signal(barrier, inc=1, device_id=(me, beside), device_id_type=MESH)
    pl.semaphore_wait(barrier, n + 1)

    arrays = ((k_in, k3, n), (v_in, v3, n), (q_in, qh, 0), (g_in, gh, 0))

    def in_copy(a, target, source):
        src, dst_ref, base = arrays[a]
        return pltpu.make_async_remote_copy(
            src_ref=src.at[0, :, pl.ds(pl.multiple_of(target * HD, HD), HD)],
            dst_ref=dst_ref.at[base + source],
            send_sem=in_send.at[a, target],
            recv_sem=in_recv.at[a, source],
            device_id=(target, frame),
            device_id_type=MESH,
        )

    def in_own(a):
        src, dst_ref, base = arrays[a]
        return pltpu.make_async_copy(
            src.at[0, :, pl.ds(pl.multiple_of(me * HD, HD), HD)],
            dst_ref.at[base + me],
            in_local.at[a],
        )

    for a in range(4):
        in_own(a).start()

    def send(first, last, a):
        def one(r, _):
            in_copy(a, peer(r, 1), me).start()
            return 0

        lax.fori_loop(first, last, one, 0)

    send(1, n, 0)
    send(1, n, 1)
    for dr in range(rows):
        for a in (2, 3):
            send(max(1, dr * cols), (dr + 1) * cols, a)

    def halo_copy(a, side, chunk):
        ref = (k3, v3)[a]
        first = chunk * cols
        return pltpu.make_async_remote_copy(
            src_ref=ref.at[pl.ds(n + first, cols)],
            dst_ref=ref.at[pl.ds((2 * n if side == 0 else 0) + first, cols)],
            send_sem=halo_send.at[a, side, chunk],
            recv_sem=halo_recv.at[a, side, chunk],
            device_id=(me, frame - 1 if side == 0 else frame + 1),
            device_id_type=MESH,
        )

    sides = ((0, has_prev, has_next), (1, has_next, has_prev))
    zero_tile = jnp.zeros((HD, HD), jnp.bfloat16)
    pst[n * slots] = zero_tile
    dst[n * slots] = zero_tile
    park[groups] = zero_tile
    parv[groups] = zero_tile

    @pl.when(jnp.logical_not(has_prev))
    def _():
        k3[0:n] = jnp.zeros((n, HD, HD), jnp.bfloat16)
        v3[0:n] = jnp.zeros((n, HD, HD), jnp.bfloat16)
        rcv[1] = jnp.zeros(rcv.shape[1:], jnp.bfloat16)

    @pl.when(jnp.logical_not(has_next))
    def _():
        k3[2 * n : 3 * n] = jnp.zeros((n, HD, HD), jnp.bfloat16)
        v3[2 * n : 3 * n] = jnp.zeros((n, HD, HD), jnp.bfloat16)
        rcv[0] = jnp.zeros(rcv.shape[1:], jnp.bfloat16)

    def pass_on(a):
        in_own(a).wait()
        for dr in range(rows):
            for dc in range(cols):
                r = dr * cols + dc
                if r > 0:
                    in_copy(a, peer(r, 1), peer(r, -1)).wait_recv()
            chunk = lax.rem(my_row - dr + rows, rows)
            for side, send_if, _ in sides:
                @pl.when(send_if)
                def _(side=side, chunk=chunk):
                    halo_copy(a, side, chunk).start()

    pass_on(0)
    mask_copy.wait()
    build_tables(mask, frame, slots, groups, (ci_v, gp_v, gq_v, last_v, bias_v, hold_v))
    moves = [
        pltpu.make_async_copy(built, table, table_sem.at[at])
        for at, (built, table) in enumerate(
            zip((ci_v, gp_v, gq_v, last_v, bias_v, hold_v), (ci, gp, gq, last, bias, hold)))
    ]
    for move in moves:
        move.start()
    pass_on(1)
    for move in moves:
        move.wait()

    for a in range(2):
        for side, _, recv_if in sides:
            @pl.when(recv_if)
            def _(a=a, side=side):
                for chunk in range(rows):
                    halo_copy(a, side, chunk).wait_recv()

    half = slots // 2
    scale = HD ** -0.5
    out_arrays = ((ot, o_out), (dqt, dq_out), (dkt, dk_out), (dvt, dv_out))

    def out_copy(a, target, source):
        tiles, out = out_arrays[a]
        return pltpu.make_async_remote_copy(
            src_ref=tiles.at[target],
            dst_ref=out.at[0, :, pl.ds(pl.multiple_of(source * HD, HD), HD)],
            send_sem=out_send.at[a, target],
            recv_sem=out_recv.at[a, source],
            device_id=(target, frame),
            device_id_type=MESH,
        )

    def out_own(a):
        tiles, out = out_arrays[a]
        return pltpu.make_async_copy(
            tiles.at[me],
            out.at[0, :, pl.ds(pl.multiple_of(me * HD, HD), HD)],
            out_local.at[a],
        )

    def within(at, size):
        return jnp.minimum(jnp.maximum(at, 0), size - 1)

    def pair_of(ref, i, jj):
        one, two = within(ci[i, 2 * jj], 3 * n), within(ci[i, 2 * jj + 1], 3 * n)
        return jnp.concatenate([ref[one], ref[two]], axis=0)

    def score_phases(i, logits):
        held = {}

        def scores():
            q = qh[i]
            top = jnp.full((HD, HD), NEG, jnp.float32)
            for jj in range(half):
                s = dot_nt(q, pair_of(k3, i, jj)) * (scale * LOG2E)
                s0 = s[:, :HD] + bias[i, 2 * jj]
                s1 = s[:, HD:] + bias[i, 2 * jj + 1]
                logits[:, jj * 2 * HD : jj * 2 * HD + HD] = s0
                logits[:, jj * 2 * HD + HD : (jj + 1) * 2 * HD] = s1
                top = jnp.maximum(top, jnp.maximum(s0, s1))
                yield
            held["highest"] = jnp.max(top, axis=1, keepdims=True)

        def output():
            highest = held["highest"]
            total = jnp.zeros((HD, HD), jnp.float32)
            o = jnp.zeros((HD, HD), jnp.float32)
            for jj in range(half):
                p = jnp.exp2(logits[:, jj * 2 * HD : (jj + 1) * 2 * HD] - highest)
                total = total + (p[:, :HD] + p[:, HD:])
                pb = p.astype(jnp.bfloat16)
                base = i * slots + 2 * jj
                pst[base] = pb[:, :HD]
                pst[base + 1] = pb[:, HD:]
                o = o + dot_nn(pb, pair_of(v3, i, jj))
                yield
            inv = 1.0 / jnp.sum(total, axis=1, keepdims=True)
            ob = (o * inv).astype(jnp.bfloat16)
            ot[i] = ob
            g = gh[i].astype(jnp.float32)
            row_dot = jnp.sum(g * ob.astype(jnp.float32), axis=1, keepdims=True)
            gt[i] = (g * inv).T.astype(jnp.bfloat16)
            qt[i] = (qh[i].astype(jnp.float32) * inv).T.astype(jnp.bfloat16)
            row_dots[i] = jnp.broadcast_to(row_dot, (HD, HD))
            inverses[i] = jnp.broadcast_to(inv, (HD, HD))

        return scores, output

    def gradients(i):
        g, row_dot = gh[i], row_dots[i]
        dq = jnp.zeros((HD, HD), jnp.float32)
        for jj in range(half):
            dp = dot_nt(g, pair_of(v3, i, jj))
            base = i * slots + 2 * jj
            ds0 = (pst[base].astype(jnp.float32) * (dp[:, :HD] - row_dot)).astype(jnp.bfloat16)
            ds1 = (pst[base + 1].astype(jnp.float32) * (dp[:, HD:] - row_dot)).astype(jnp.bfloat16)
            dst[base] = ds0
            dst[base + 1] = ds1
            dq = dq + dot_nn(jnp.concatenate([ds0, ds1], axis=1), pair_of(k3, i, jj))
            yield
        dqt[i] = (dq * (inverses[i] * scale)).astype(jnp.bfloat16)

    def leave_block(a, b, tiles):
        for u in range(BLOCK):

            def leave(u=u):
                out_copy(a, tiles[u], me).start()

            if u > 0:
                leave()
            else:
                pl.when(b > 0)(leave)

                @pl.when(b == 0)
                def _():
                    out_own(a).start()

    def score_block(b, _):
        tiles = [peer(b * BLOCK + u, -1) for u in range(BLOCK)]
        for u in range(BLOCK):
            r = b * BLOCK + u

            def came(r=r, u=u):
                for a in (2, 3):
                    in_copy(a, peer(r, 1), tiles[u]).wait_recv()

            if u > 0:
                came()
            else:
                pl.when(b > 0)(came)

                @pl.when(b == 0)
                def _():
                    for a in (2, 3):
                        in_own(a).wait()

        steps = [score_phases(tiles[u], sbuf.at[u]) for u in range(BLOCK)]
        together(steps[0][0]())
        for u in range(BLOCK):
            after = [steps[u + 1][0]()] if u + 1 < BLOCK else []
            together(steps[u][1](), *after)
        leave_block(0, b, tiles)
        return 0

    def gradient_block(b, _):
        tiles = [peer(b * BLOCK + u, -1) for u in range(BLOCK)]
        for u in range(0, BLOCK, 2):
            together(gradients(tiles[u]), gradients(tiles[u + 1]))
        leave_block(1, b, tiles)
        return 0

    def key_side(a):
        left, right, par = ((qt, dst, park), (gt, pst, parv))[a]

        def row(y, acc):
            for u in range(8):
                whose = [within(gq[y, 2 * u + k], n) for k in range(2)]
                which = [within(gp[y, 2 * u + k], n * slots + 1) for k in range(2)]
                term = dot_nn(
                    jnp.concatenate([left[k] for k in whose], axis=1),
                    jnp.concatenate([right[k] for k in which], axis=0))
                acc = acc * hold[y, 2 * u] + term
                par[8 * y + u] = (acc * scale if a == 0 else acc).astype(jnp.bfloat16)
            return acc

        lines = groups // 8
        unroll = 3 if lines % 3 == 0 else 1
        lax.fori_loop(0, lines, row, jnp.zeros((HD, HD), jnp.float32), unroll=unroll)

    def tile_of(a, t):
        return (park, parv)[a][within(last[0, (frame - 1) * n + t], groups + 1)].T

    def gr_copy(a, side, i):
        return pltpu.make_async_remote_copy(
            src_ref=snd.at[side, a, i],
            dst_ref=rcv.at[side, a, i],
            send_sem=gr_send.at[side, a, i],
            recv_sem=gr_recv.at[side, a, i],
            device_id=(me, frame - 1 if side == 0 else frame + 1),
            device_id_type=MESH,
        )

    def neighbour_terms(a):
        def four(b, _):
            tiles = [peer(b * BLOCK + u, -1) for u in range(BLOCK)]
            for side, send_if, _ in sides:
                @pl.when(send_if)
                def _(side=side):
                    for i in tiles:
                        snd[side, a, i] = tile_of(a, i if side == 0 else 2 * n + i)
                    for i in tiles:
                        gr_copy(a, side, i).start()
            return 0

        lax.fori_loop(0, n // BLOCK, four, 0)

    def finish(a):
        def four(b, _):
            tiles = [peer(b * BLOCK + u, -1) for u in range(BLOCK)]
            for side, _, recv_if in sides:
                @pl.when(recv_if)
                def _(side=side):
                    for i in tiles:
                        gr_copy(a, side, i).wait_recv()
            for i in tiles:
                tot = tile_of(a, n + i).astype(jnp.float32)
                tot = tot + rcv[0, a, i].astype(jnp.float32) + rcv[1, a, i].astype(jnp.float32)
                (dkt, dvt)[a][i] = tot.astype(jnp.bfloat16)
            leave_block(2 + a, b, tiles)
            return 0

        lax.fori_loop(0, n // BLOCK, four, 0)

    lax.fori_loop(0, n // BLOCK, score_block, 0)
    key_side(1)
    neighbour_terms(1)
    lax.fori_loop(0, n // BLOCK, gradient_block, 0)
    finish(1)
    key_side(0)
    neighbour_terms(0)
    finish(0)

    for a in range(4):
        out_own(a).wait()

        def settle(r, _, a=a):
            there, back = peer(r, 1), peer(r, -1)
            in_copy(a, there, me).wait_send()
            out_copy(a, back, me).wait_send()
            out_copy(a, there, back).wait_recv()
            return 0

        lax.fori_loop(1, n, settle, 0)
    for side, send_if, _ in sides:
        @pl.when(send_if)
        def _(side=side):
            for a in range(2):
                for chunk in range(rows):
                    halo_copy(a, side, chunk).wait_send()

            def settle_terms(i, _):
                for a in range(2):
                    gr_copy(a, side, i).wait_send()
                return 0

            lax.fori_loop(0, n, settle_terms, 0)


def body(shape, queries, keys, values, out_grad, tile_mask):
    rows, cols, frames = shape
    n = rows * cols
    slots = min(18, 3 * n)
    groups = -(-(n * slots + 3 * n) // 16) * 8
    lines = -(-groups // 256) * 32
    any_ = pl.BlockSpec(memory_space=pl.ANY)
    tile = lambda *lead: pltpu.VMEM(lead + (HD, HD), jnp.bfloat16)
    dma = pltpu.SemaphoreType.DMA
    table_shapes = (
        ((n, HD), jnp.int32), ((lines, HD), jnp.int32), ((lines, HD), jnp.int32),
        ((8, frames * n), jnp.int32), ((n, HD), jnp.float32), ((lines, HD), jnp.float32))
    return pl.pallas_call(
        functools.partial(kernel, rows, cols, slots, groups, frames),
        out_shape=[jax.ShapeDtypeStruct(queries.shape, jnp.bfloat16)] * 4,
        in_specs=[any_] * 5,
        out_specs=[any_] * 4,
        scratch_shapes=[
            tile(3 * n), tile(3 * n), tile(n), tile(n),
            pltpu.VMEM((BLOCK, HD, slots * HD), jnp.float32),
            pltpu.VMEM((n, HD, HD), jnp.float32), pltpu.VMEM((n, HD, HD), jnp.float32),
            tile(n * slots + 1), tile(n * slots + 1),
            tile(n), tile(n),
            tile(groups + 1), tile(groups + 1),
            tile(n), tile(n), tile(2, 2, n), tile(2, 2, n), tile(n), tile(n),
            pltpu.VMEM((n, frames * n), jnp.int32),
            *[pltpu.VMEM(dims, kind) for dims, kind in table_shapes],
            *[pltpu.SMEM(dims, kind) for dims, kind in table_shapes],
            dma, dma((6,)),
            dma((4, n)), dma((4, n)), dma((4,)),
            dma((2, 2, rows)), dma((2, 2, rows)),
            dma((2, 2, n)), dma((2, 2, n)),
            dma((4, n)), dma((4, n)), dma((4,)),
        ],
        compiler_params=pltpu.CompilerParams(
            collective_id=0, has_side_effects=True, vmem_limit_bytes=56 * 1024 * 1024),
    )(queries, keys, values, out_grad, tile_mask)


def solution(mesh):
    n, frames = mesh.shape["seq"], mesh.shape["ctx"]
    cols = 4 if n % 4 == 0 and n > 4 else 2
    shape = (n // cols, cols, frames)
    data = P("ctx", "seq", None)
    return jax.shard_map(
        functools.partial(body, shape),
        mesh=mesh,
        in_specs=(data,) * 4 + (P("seq", None, None, None),),
        out_specs=(data,) * 4,
        check_vma=False,
    )
```
